128 devices in a mesh: pool: 16 (over x, y), grp: 8 (over z, core).
Axes of the slice: x: 4, y: 4, z: 4, core: 2. Of those that a mesh axis runs over, the one named last changes fastest.
Arguments:
- queries: bfloat16 [256, 4096], P(('pool', 'grp')), may hold values from -6 to 6
- key_cache: bfloat16 [256, 1024, 256], P(('pool', 'grp')), may hold values from -8 to 8
- value_cache: bfloat16 [256, 1024, 256], P(('pool', 'grp')), may hold values from -24 to 24
- lengths: int32 [256], P(('pool', 'grp')), may hold values from 128 to 1024, as said below
- residual: bfloat16 [256, 4096], P('pool', 'grp'), may hold values from -6 to 6
- out_proj: bfloat16 [4096, 4096], P(None, 'grp'), may hold values from -0.09375 to 0.09375
- norm_gain: float32 [4096], P('grp'), may hold values from 0.1 to 1.9
- expert_ids: int32 [256, 8], P('pool'), may hold values from 0 to 63, all different within a row; in each aligned block of 16 rows (0 to 15, 16 to 31, ...) at most 4 rows name the same one
- route_weights: float32 [256, 8], P('pool'), may hold values from 0.05 to 1
- w_gate: bfloat16 [64, 4096, 1536], P('pool', None, 'grp'), may hold values from -0.09375 to 0.09375
- w_up: bfloat16 [64, 4096, 1536], P('pool', None, 'grp'), may hold values from -0.09375 to 0.09375
- w_down: bfloat16 [64, 1536, 4096], P('pool', 'grp'), may hold values from -0.15625 to 0.15625
Outputs:
- layer_out: bfloat16 [256, 4096], P('pool', 'grp')
The draws below stay inside these ranges and needn't reach their ends.
Inputs may be any that keep to these rules, and one draw needn't show every extreme that they name: `expert_ids`: among the 16 rows of one index of pool (aligned blocks of rows) no expert is named by more than 4 routes; a row names 8 different experts. `lengths`: some row has exactly 1024 and some row exactly 128.
All inputs are finite; a program needn't handle non-finite values.
Results may differ from the reference program's by a relative error of at most 0.018.
Values may be sent and summed in bfloat16 or wider, within the bound.
No kernel may reach another device: no remote copies, remote signals or barrier semaphores. Data moves between devices by JAX's collectives and lax.ppermute only.
A program may use at most 128 MiB of HBM per device.

```python
import math
import jax
import jax.numpy as jnp
import numpy as np
from jax import lax

D = 4096
HEADS = 32
KV_HEADS = 2
HEAD = 128
FF = 1536
TOP = 8
CAP = 4
ROWS_DEV = 16
LEN = 1024
TOKENS = 256
EXPERTS = 64
N_POOL = 16


def draw_queries(key, part):
    key = jax.random.fold_in(key, 11)
    shape = (TOKENS, KV_HEADS, HEADS // KV_HEADS, HEAD)
    entries = jnp.clip(jax.random.normal(key, shape), -6.0, 6.0)
    return entries.reshape(TOKENS, HEADS * HEAD).astype(jnp.bfloat16)


def draw_key_cache(key, part):
    key = jax.random.fold_in(key, 12)
    shape = (TOKENS, LEN, KV_HEADS, HEAD)
    entries = jnp.clip(jax.random.normal(key, shape), -6.0, 6.0)
    return entries.reshape(TOKENS, LEN, KV_HEADS * HEAD).astype(jnp.bfloat16)


def draw_lengths(key, part):
    key = jax.random.fold_in(key, 13)
    draw_key, pick_key = jax.random.split(key)
    shortest = LEN // 8
    drawn = jax.random.randint(draw_key, (TOKENS,), shortest, LEN + 1)
    picked = jax.random.randint(pick_key, (), 0, TOKENS)
    places = jnp.arange(TOKENS)
    drawn = jnp.where(places == picked, LEN, drawn)
    drawn = jnp.where(places == (picked + 1) % TOKENS, shortest, drawn)
    return drawn.astype(jnp.int32)


def level_of(rng, dims, shards, low, high):
    factor_of = 1.0
    for axis_at, shards_of in shards:
        draws = jax.random.uniform(jax.random.fold_in(jax.random.fold_in(rng, 6), axis_at), (shards_of,), jnp.float32, low / len(shards), high / len(shards))
        factor_of = factor_of * jnp.repeat(jnp.exp(draws), dims[axis_at] // shards_of).reshape((-1,) + (1,) * (len(dims) - 1 - axis_at))
    return factor_of


def routed_block(rng, own, number, rows, number_of, top, reach, slope):
    sequence = jax.random.permutation(rng, number_of)
    heavy_load, common = portions_of(number_of, rows * top, reach, slope, True), portions_of(number_of, rows * top, reach, slope, False)
    places = jnp.arange(number_of)

    def named(sizes, offset_by):
        used = int((sizes > 0).sum())
        fixed = max(1, used // 4)
        shifted = fixed + (places - fixed + offset_by * (used - fixed)) % max(1, number_of - fixed)
        return jnp.zeros((number_of,), jnp.int32).at[sequence[jnp.where(places < fixed, places, shifted)]].set(jnp.asarray(sizes, jnp.int32))

    sizes = jnp.where(number % 4 == 0, named(heavy_load, number // 4), named(common, number - number // 4 - 1))
    mixed = jax.random.permutation(jax.random.fold_in(own, 3), number_of)
    source_of, receiver = mixed[0:number_of // 2 * 2:2], mixed[1:number_of // 2 * 2:2]
    slack = jnp.minimum(sizes[source_of] - 1, reach - sizes[receiver]) // 2
    slack = jnp.where((source_of == sequence[0]) | (receiver == sequence[0]) | (sizes[receiver] == 0), 0, jnp.maximum(slack, 0))
    shifted = jax.random.randint(jax.random.fold_in(own, 4), (number_of // 2,), 0, 1 << 20) % (slack + 1)
    sizes = sizes.at[source_of].add(-shifted).at[receiver].add(shifted)
    items = jnp.searchsorted(jnp.cumsum(sizes), jnp.arange(rows * top), side="right").astype(jnp.int32)
    listing = items.reshape(top, rows).T
    listing = listing[jax.random.permutation(jax.random.fold_in(own, 1), rows)]
    offset_by = jax.random.randint(jax.random.fold_in(own, 2), (rows, 1), 0, top)
    return jnp.take_along_axis(listing, (jnp.arange(top)[None, :] + offset_by) % top, axis=1)


def portions_of(count, total, reach, lean, full):
    weights = [(1 << 20) // math.isqrt(standing ** lean) + 1 for standing in range(1, count + 1)]
    largest = reach if full else min(reach, max(-(-total // count), total * weights[0] // sum(weights)))
    least = 1 if total - largest >= count - 1 else 0
    counts, rest = [largest] + [least] * (count - 1), total - largest - least * (count - 1)
    while rest > 0:
        free = [i for i in range(1, count) if counts[i] < largest] or [i for i in range(1, count) if counts[i] < reach]
        mass, left = sum([weights[i] for i in free]), rest
        for i in free:
            more = min(reach - counts[i], max(1, left * weights[i] // mass), rest)
            counts[i] = counts[i] + more
            rest = rest - more
    return np.array(counts)


def bell_draw(stream_key, shape, deviation, limit, cuts=(), kind=jnp.bfloat16):
    level = level_of(stream_key, shape, cuts, -0.22, 0.18) if cuts else 1.0
    values = jax.random.normal(stream_key, shape, jnp.float32) * deviation * level
    return jnp.minimum(jnp.maximum(values, -limit), limit).astype(kind)


def setup_inputs(seed: int = 0) -> dict:
    arg_keys = jax.random.split(jax.random.key(seed), 13)
    queries = draw_queries(jax.random.fold_in(arg_keys[12], 71), 0)
    key_cache = draw_key_cache(jax.random.fold_in(arg_keys[12], 71), 0)
    value_cache = bell_draw(arg_keys[2], (TOKENS, LEN, KV_HEADS * HEAD), 4.0, 24.0, ((0, 128),))
    lengths = draw_lengths(jax.random.fold_in(arg_keys[12], 71), 0)
    residual = bell_draw(arg_keys[4], (TOKENS, D), 1.0, 6.0, ((0, 16), (1, 8)))
    out_proj = bell_draw(arg_keys[5], (HEADS * HEAD, D), (HEADS * HEAD) ** -0.5, 0.09375, ((1, 8),))
    norm_gain = jnp.clip(1.0 + 0.18 * jax.random.normal(arg_keys[6], (D,), jnp.float32), 0.1, 1.9)
    expert_ids_keys = jax.random.split(jax.random.fold_in(arg_keys[7], 1), TOKENS // ROWS_DEV)
    expert_ids_turns = jax.random.permutation(jax.random.fold_in(arg_keys[7], 3), TOKENS // ROWS_DEV)
    expert_ids = jax.vmap(lambda own, number: routed_block(jax.random.fold_in(arg_keys[7], 2), own, number, ROWS_DEV, EXPERTS, TOP, CAP, 2))(expert_ids_keys, expert_ids_turns).reshape((TOKENS, TOP))
    route_weights = jnp.clip(jnp.exp(math.log(1.0) - 2.9957323 * jax.random.uniform(arg_keys[8], (TOKENS, TOP), jnp.float32) ** level_of(arg_keys[8], (TOKENS, TOP), ((0, 16),), -0.2, 0.2)), 0.05, 1.0)
    w_gate = bell_draw(arg_keys[9], (EXPERTS, D, FF), D ** -0.5, 0.09375, ((0, 16), (2, 8)))
    w_up = bell_draw(arg_keys[10], (EXPERTS, D, FF), D ** -0.5, 0.09375, ((0, 16), (2, 8)))
    w_down = bell_draw(arg_keys[11], (EXPERTS, FF, D), FF ** -0.5, 0.15625, ((0, 16), (1, 8)))
    return {"queries": queries, "key_cache": key_cache, "value_cache": value_cache, "lengths": lengths, "residual": residual, "out_proj": out_proj, "norm_gain": norm_gain, "expert_ids": expert_ids, "route_weights": route_weights, "w_gate": w_gate, "w_up": w_up, "w_down": w_down}


def reference(queries, key_cache, value_cache, lengths, residual, out_proj, norm_gain, expert_ids, route_weights, w_gate, w_up, w_down):
    row_count = queries.shape[0]
    per_group = HEADS // KV_HEADS
    query_heads = queries.astype(jnp.float32).reshape(row_count, KV_HEADS, per_group, HEAD)
    key_heads = key_cache.astype(jnp.float32).reshape(row_count, LEN, KV_HEADS, HEAD)
    value_heads = value_cache.astype(jnp.float32).reshape(row_count, LEN, KV_HEADS, HEAD)
    scores = jnp.einsum('rkhd,rpkd->rkhp', query_heads, key_heads, precision=lax.Precision.HIGHEST) / math.sqrt(HEAD)
    live_mask = (jnp.arange(LEN, dtype=jnp.int32)[None, :] < lengths[:, None])[:, None, None, :]
    peak = lax.optimization_barrier(jnp.max(jnp.where(live_mask, scores, -1e+30), axis=3))
    probs = jnp.where(live_mask, jnp.exp(scores - peak[..., None]), 0.0)
    weight_sum = lax.optimization_barrier(jnp.sum(probs, axis=3))
    summed = jnp.einsum('rkhp,rpkd->rkhd', probs, value_heads, precision=lax.Precision.HIGHEST)
    attended = (summed / weight_sum[..., None]).reshape(row_count, HEADS * HEAD).astype(jnp.bfloat16)
    stream = (residual.astype(jnp.float32) + jnp.dot(attended, out_proj, preferred_element_type=jnp.float32)).astype(jnp.bfloat16)
    widened = stream.astype(jnp.float32)
    scaling = lax.rsqrt(lax.optimization_barrier(jnp.mean(widened * widened, axis=1)) + 1e-06)
    moe_in = (widened * scaling[:, None] * norm_gain[None, :]).astype(jnp.bfloat16)
    flat_ids = expert_ids.reshape(-1)
    route_rows = jnp.arange(row_count * TOP, dtype=jnp.int32) // TOP
    flat_weights = route_weights.reshape(-1)
    most_routes = N_POOL * CAP

    def one_expert(packed):
        number, gate_mat, up_mat, down_mat = packed
        order = jnp.argsort((flat_ids != number).astype(jnp.int32), stable=True)[:most_routes].astype(jnp.int32)
        valid = flat_ids[order] == number
        taken_rows = route_rows[order]
        taken = moe_in[taken_rows]
        gate_act = jnp.dot(taken, gate_mat, preferred_element_type=jnp.float32)
        up_act = jnp.dot(taken, up_mat, preferred_element_type=jnp.float32)
        hidden = (jax.nn.silu(gate_act) * up_act).astype(jnp.bfloat16)
        expert_out = jnp.dot(hidden, down_mat, preferred_element_type=jnp.float32)
        weighting = jnp.where(valid, flat_weights[order], 0.0)
        return (expert_out * weighting[:, None], taken_rows)
    numbers = jnp.arange(EXPERTS, dtype=jnp.int32)
    contribution, targets = lax.map(one_expert, (numbers, w_gate, w_up, w_down))
    moe_sum = jnp.zeros((row_count, D), jnp.float32).at[targets.reshape(-1)].add(contribution.reshape(-1, D))
    return (stream.astype(jnp.float32) + moe_sum).astype(jnp.bfloat16)
```

```python
import functools
import math

import jax
import jax.numpy as jnp
from jax import lax
from jax.experimental import pallas as pl
from jax.experimental.pallas import tpu as pltpu
from jax.sharding import PartitionSpec as P

D = 4096
KV_HEADS = 2
HEAD = 128
SIDE = 4
CORES = 2
COLS = D // (SIDE * CORES)
EXTRA = 128
IDS, HI, MID, LO, SQ = 0, 8, 16, 24, 32
F32 = jnp.float32
BF16 = jnp.bfloat16
NT = (((1,), (1,)), ((), ()))
VMEM = pl.BlockSpec(memory_space=pltpu.VMEM)
SMEM = pl.BlockSpec(memory_space=pltpu.SMEM)


def params(mib):
    return pltpu.CompilerParams(vmem_limit_bytes=mib * 1024 * 1024)


def split3(value):
    hi = value.astype(BF16).astype(F32)
    mid = (value - hi).astype(BF16).astype(F32)
    lo = value - hi - mid
    return hi, mid, lo


def shift_x(k):
    return [(x * SIDE + y, (x + k) % SIDE * SIDE + y) for x in range(SIDE) for y in range(SIDE)]


def shift_y(k):
    return [(x * SIDE + y, x * SIDE + (y + k) % SIDE) for x in range(SIDE) for y in range(SIDE)]


def shift_z(k):
    return [(z * CORES + c, (z + k) % SIDE * CORES + c) for z in range(SIDE) for c in range(CORES)]


OTHER_CORE = [(z * CORES + c, z * CORES + 1 - c) for z in range(SIDE) for c in range(CORES)]


def spread(block, axis, shift):
    return [block] + [lax.ppermute(block, axis, shift(k)) for k in range(1, SIDE)]


def give_back(blocks, axis, shift):
    return [blocks[0]] + [lax.ppermute(blocks[k], axis, shift(-k)) for k in range(1, SIDE)]


def attention_kernel(len_ref, q_ref, k_ref, v_ref, out_ref, q_rows, out_rows):
    rows = q_ref.shape[0]
    positions = k_ref.shape[1]
    heads = q_ref.shape[1] // HEAD
    per_group = heads // KV_HEADS
    queries = q_ref[...].astype(F32)
    for r in range(rows):
        for h in range(heads):
            q_rows[r * heads + h : r * heads + h + 1, :] = queries[
                r : r + 1, h * HEAD : (h + 1) * HEAD
            ]
    spots = lax.broadcasted_iota(jnp.int32, (per_group, positions), 1)
    for r in range(rows):
        live = spots < len_ref[r]
        for g in range(KV_HEADS):
            first = r * heads + g * per_group
            q = q_rows[first : first + per_group, :].astype(BF16)
            keys = k_ref[r, :, g * HEAD : (g + 1) * HEAD]
            scores = lax.dot_general(q, keys, NT, preferred_element_type=F32) / math.sqrt(HEAD)
            scores = jnp.where(live, scores, -1e30)
            peak = jnp.max(scores, axis=1, keepdims=True)
            probs = jnp.where(live, jnp.exp(scores - peak), 0.0)
            weight_sum = jnp.sum(probs, axis=1, keepdims=True)
            values = v_ref[r, :, g * HEAD : (g + 1) * HEAD]
            summed = jnp.dot(probs.astype(BF16), values, preferred_element_type=F32)
            summed = summed / weight_sum
            for j in range(per_group):
                h = g * per_group + j
                out_rows[r : r + 1, h * HEAD : (h + 1) * HEAD] = summed[j : j + 1, :]
    out_ref[...] = out_rows[...].astype(BF16)


def attention(lengths, queries, keys, values):
    rows, width = queries.shape
    return pl.pallas_call(
        attention_kernel,
        out_shape=jax.ShapeDtypeStruct((rows, width), BF16),
        in_specs=[SMEM, VMEM, VMEM, VMEM],
        out_specs=VMEM,
        scratch_shapes=[
            pltpu.VMEM((rows * width // HEAD, HEAD), F32),
            pltpu.VMEM((rows, width), F32),
        ],
        compiler_params=params(16),
        name="attention",
    )(lengths, queries, keys, values)


def routes_kernel(ids_ref, weights_ref, out_ref):
    top = ids_ref.shape[0]
    lane = lax.broadcasted_iota(jnp.int32, (top, EXTRA), 1)
    slot = lax.broadcasted_iota(jnp.int32, (top, EXTRA), 0)
    hi, mid, lo = split3(weights_ref[...])
    total = None
    for piece, start in ((ids_ref[...].astype(F32), IDS), (hi, HI), (mid, MID), (lo, LO)):
        place = (lane == slot + start).astype(BF16)
        part = lax.dot_general(
            piece.astype(BF16), place, (((0,), (0,)), ((), ())), preferred_element_type=F32
        )
        total = part if total is None else total + part
    out_ref[...] = total.astype(BF16)


def routes(ids, weights):
    return pl.pallas_call(
        routes_kernel,
        out_shape=jax.ShapeDtypeStruct((ids.shape[1], EXTRA), BF16),
        in_specs=[VMEM, VMEM],
        out_specs=VMEM,
        name="routes",
    )(ids, weights)


def with_squares(extra, squares):
    lane = lax.broadcasted_iota(jnp.int32, extra.shape, 1)
    for i, piece in enumerate(split3(squares)):
        extra = jnp.where(lane == SQ + i, piece, extra)
    return extra


def squares_of(extra):
    lane = lax.broadcasted_iota(jnp.int32, extra.shape, 1)
    return jnp.sum(
        jnp.where((lane >= SQ) & (lane < SQ + 3), extra, 0.0), axis=1, keepdims=True
    )


def stream_kernel(
    a0, a1, a2, a3, w_ref, residual_ref, gain_ref, extra_ref, stream_ref, unit_ref, rows_ref
):
    part = a0.shape[0]
    for k, a in enumerate((a0, a1, a2, a3)):
        rows_ref[k * part : (k + 1) * part, :] = a[...].astype(F32)
    mixed = jnp.dot(rows_ref[...].astype(BF16), w_ref[...], preferred_element_type=F32)
    rows = SIDE * part
    half = part // CORES
    me = lax.axis_index("grp")
    z, c = me // CORES, me % CORES
    here = lax.broadcasted_iota(jnp.int32, (rows, rows), 1)
    wanted = lax.broadcasted_iota(jnp.int32, (rows, rows), 0)
    slot, within = here // part, here % part
    owner = (z - slot + SIDE) % SIDE * CORES + (c + within // half) % CORES
    order = (wanted == owner * half + within % half).astype(F32)
    mixed = jnp.dot(order, mixed, precision=lax.Precision.HIGHEST, preferred_element_type=F32)
    stream = (residual_ref[...].astype(F32) + mixed).astype(BF16)
    stream_ref[...] = stream
    widened = stream.astype(F32)
    unit_ref[:, :COLS] = (widened * gain_ref[...]).astype(BF16)
    squares = jnp.sum(widened * widened, axis=1, keepdims=True)
    unit_ref[:, COLS:] = with_squares(extra_ref[...].astype(F32), squares).astype(BF16)


def make_stream(parts, out_proj, residual, gain, extra):
    rows = residual.shape[0]
    return pl.pallas_call(
        stream_kernel,
        out_shape=[
            jax.ShapeDtypeStruct((rows, COLS), BF16),
            jax.ShapeDtypeStruct((rows, COLS + EXTRA), BF16),
        ],
        in_specs=[VMEM] * 8,
        out_specs=[VMEM, VMEM],
        scratch_shapes=[pltpu.VMEM((rows, D), F32)],
        compiler_params=params(16),
        name="stream",
    )(*parts, out_proj, residual, gain, extra)


def pack_kernel(u0, u1, u2, u3, out_ref):
    squares = None
    for k, unit in enumerate((u0, u1, u2, u3)):
        out_ref[:, k * COLS : (k + 1) * COLS] = unit[:, :COLS]
        part = squares_of(unit[:, COLS:].astype(F32))
        squares = part if squares is None else squares + part
    out_ref[:, SIDE * COLS :] = with_squares(u0[:, COLS:].astype(F32), squares).astype(BF16)


def pack(units):
    return pl.pallas_call(
        pack_kernel,
        out_shape=jax.ShapeDtypeStruct((units[0].shape[0], SIDE * COLS + EXTRA), BF16),
        in_specs=[VMEM] * SIDE,
        out_specs=VMEM,
        name="pack",
    )(*units)


def column_block(z, k, c):
    return pl.ds(pl.multiple_of(((z - k + SIDE) % SIDE * CORES + c) * COLS, COLS), COLS)


def experts_kernel(
    o0, o1, o2, o3, t0, t1, t2, t3, gate_ref, up_ref, down_ref, hidden_ref, out_ref, x_ref
):
    me = lax.axis_index("grp")
    z, c = me // CORES, me % CORES
    first = lax.axis_index("pool") * (gate_ref.shape[0] // EXPERT_COLS)
    rows = o0.shape[0]
    scales = []
    mixes = []
    for kx, (own, other) in enumerate(((o0, t0), (o1, t1), (o2, t2), (o3, t3))):
        for k in range(SIDE):
            for half, parity in ((own, c), (other, 1 - c)):
                x_ref[kx * rows : (kx + 1) * rows, column_block(z, k, parity)] = half[
                    :, k * COLS : (k + 1) * COLS
                ]
        extra = own[:, SIDE * COLS :].astype(F32)
        squares = squares_of(extra) + squares_of(other[:, SIDE * COLS :].astype(F32))
        scales.append(lax.rsqrt(squares / D + 1e-06))
        lane = lax.broadcasted_iota(jnp.int32, extra.shape, 1)
        weights = (
            pltpu.roll(extra, EXTRA - HI, 1)
            + pltpu.roll(extra, EXTRA - MID, 1)
            + pltpu.roll(extra, EXTRA - LO, 1)
        )
        picked = []
        for e in range(gate_ref.shape[0] // EXPERT_COLS):
            mine = (lane < HI) & (extra == (first + e).astype(F32))
            picked.append(jnp.sum(jnp.where(mine, weights, 0.0), axis=1, keepdims=True))
        mixes.append(picked)
    scale = jnp.concatenate(scales, axis=0)
    x = x_ref[...]
    gate = lax.dot_general(x, gate_ref[...], NT, preferred_element_type=F32) * scale
    up = lax.dot_general(x, up_ref[...], NT, preferred_element_type=F32) * scale
    column = lax.broadcasted_iota(jnp.int32, gate.shape, 1)
    mix = None
    for e in range(len(mixes[0])):
        one = jnp.concatenate([m[e] for m in mixes], axis=0)
        mix = one if mix is None else jnp.where(column < e * EXPERT_COLS, mix, one)
    hidden = (gate / (1.0 + jnp.exp(-gate)) * up * mix).astype(BF16)
    hidden_ref[...] = hidden
    for k in range(SIDE):
        out_ref[:, k * COLS : (k + 1) * COLS] = jnp.dot(
            hidden, down_ref[:, column_block(z, k, 1 - c)], preferred_element_type=F32
        ).astype(BF16)


EXPERT_COLS = 192


def experts(own, other, gate, up, down):
    rows = SIDE * own[0].shape[0]
    width = gate.shape[0]
    return pl.pallas_call(
        experts_kernel,
        out_shape=[
            jax.ShapeDtypeStruct((rows, width), BF16),
            jax.ShapeDtypeStruct((rows, SIDE * COLS), BF16),
        ],
        in_specs=[VMEM] * 11,
        out_specs=[VMEM, VMEM],
        scratch_shapes=[pltpu.VMEM((rows, D), BF16)],
        compiler_params=params(20),
        cost_estimate=pl.CostEstimate(
            flops=5 * rows * width * D, bytes_accessed=6 * width * D, transcendentals=rows * width
        ),
        name="experts",
    )(*own, *other, gate, up, down)


def down_kernel(hidden_ref, down_ref, out_ref):
    me = lax.axis_index("grp")
    z, c = me // CORES, me % CORES
    for k in range(SIDE):
        out_ref[:, k * COLS : (k + 1) * COLS] = jnp.dot(
            hidden_ref[...], down_ref[:, column_block(z, k, c)], preferred_element_type=F32
        ).astype(BF16)


def down_own(hidden, down):
    rows, width = hidden.shape
    return pl.pallas_call(
        down_kernel,
        out_shape=jax.ShapeDtypeStruct((rows, SIDE * COLS), BF16),
        in_specs=[VMEM, VMEM],
        out_specs=VMEM,
        compiler_params=params(20),
        cost_estimate=pl.CostEstimate(
            flops=rows * width * D, bytes_accessed=2 * width * D, transcendentals=0
        ),
        name="down_own",
    )(hidden, down)


def on_device(
    queries,
    key_cache,
    value_cache,
    lengths,
    residual,
    out_proj,
    norm_gain,
    expert_ids,
    route_weights,
    w_gate,
    w_up,
    w_down,
):
    gate = jnp.swapaxes(w_gate, 1, 2).reshape(-1, D)
    up = jnp.swapaxes(w_up, 1, 2).reshape(-1, D)
    down = w_down.reshape(-1, D)
    gate, up, down, out_proj = (
        pltpu.with_memory_space_constraint(w, pltpu.VMEM) for w in (gate, up, down, out_proj)
    )
    extra = routes(expert_ids.T, route_weights.T)
    attended = attention(lengths, queries, key_cache, value_cache)
    pair = jnp.concatenate([attended, lax.ppermute(attended, "grp", OTHER_CORE)], axis=0)
    parts = spread(pair, "grp", shift_z)
    stream, unit = make_stream(parts, out_proj, residual, norm_gain[None, :], extra)
    column = pack(spread(unit, "grp", shift_z))
    plane = jnp.concatenate(spread(column, "pool", shift_y), axis=0)
    own = spread(plane, "pool", shift_x)
    other = [lax.ppermute(block, "grp", OTHER_CORE) for block in own]
    hidden, theirs = experts(own, other, gate, up, down)
    came = lax.ppermute(theirs, "grp", OTHER_CORE)
    mine = down_own(hidden, down)
    total = (mine.astype(F32) + came.astype(F32)).astype(BF16)
    for axis, shift in (("pool", shift_x), ("pool", shift_y)):
        slots = give_back(jnp.split(total, SIDE, axis=0), axis, shift)
        total = sum(s.astype(F32) for s in slots).astype(BF16)
    slots = give_back(jnp.split(total, SIDE, axis=1), "grp", shift_z)
    combined = sum(s.astype(F32) for s in slots)
    return (stream.astype(F32) + combined).astype(BF16)


def solution(mesh):
    in_specs = (
        P(("pool", "grp"), None),
        P(("pool", "grp"), None, None),
        P(("pool", "grp"), None, None),
        P(("pool", "grp")),
        P("pool", "grp"),
        P(None, "grp"),
        P("grp"),
        P("pool", None),
        P("pool", None),
        P("pool", None, "grp"),
        P("pool", None, "grp"),
        P("pool", "grp", None),
    )
    return jax.shard_map(
        on_device, mesh=mesh, in_specs=in_specs, out_specs=P("pool", "grp"), check_vma=False
    )
```

```python
import math

import jax
import jax.numpy as jnp
from jax import lax
from jax.experimental import pallas as pl
from jax.experimental.pallas import tpu as pltpu
from jax.sharding import Mesh
from jax.sharding import PartitionSpec as P

D = 4096
KV_HEADS = 2
HEAD = 128
LANES = 128
SIDE = 4
CORES = 2
PLACES = SIDE * SIDE
COLS = D // (SIDE * CORES)
CHUNKS = COLS // LANES
ROWS = 16
UNIT = CHUNKS * ROWS
EXTRA = 8
IDS, HI, MID, LO, SQ = 0, ROWS, 2 * ROWS, 3 * ROWS, 4 * ROWS
EXPERT_COLS = 192
F32 = jnp.float32
BF16 = jnp.bfloat16
NT = (((1,), (1,)), ((), ()))
VMEM = pl.BlockSpec(memory_space=pltpu.VMEM)
ANY = pl.BlockSpec(memory_space=pl.ANY)


def params(mib):
    return pltpu.CompilerParams(vmem_limit_bytes=mib * 1024 * 1024)


def split3(value):
    hi = value.astype(BF16).astype(F32)
    mid = (value - hi).astype(BF16).astype(F32)
    lo = value - hi - mid
    return hi, mid, lo


SWAP = [(0, 1), (1, 0)]


def swap(block):
    return lax.ppermute(block, "c", SWAP)


def spread_z(block):
    return [block] + [
        lax.ppermute(block, "z", [(i, (i + k) % SIDE) for i in range(SIDE)])
        for k in range(1, SIDE)
    ]


def attention_kernel(
    len_hbm, q_hbm, k_hbm, v_hbm, out_ref, lens, q_ref, k_ref, v_ref, q_rows, out_rows, sems
):
    rows, width = q_ref.shape
    positions = k_ref.shape[1]
    heads = width // HEAD
    per_group = heads // KV_HEADS
    len_copy = pltpu.make_async_copy(len_hbm, lens, sems.at[0])
    q_copy = pltpu.make_async_copy(q_hbm, q_ref, sems.at[1])
    k_copies = [
        pltpu.make_async_copy(k_hbm.at[r], k_ref.at[r], sems.at[2 + r]) for r in range(rows)
    ]
    v_copies = [
        pltpu.make_async_copy(v_hbm.at[r], v_ref.at[r], sems.at[2 + rows + r])
        for r in range(rows)
    ]
    q_copy.start()
    len_copy.start()
    for r in range(rows):
        k_copies[r].start()
        v_copies[r].start()
    q_copy.wait()
    queries = q_ref[...].astype(F32)
    for r in range(rows):
        for h in range(heads):
            q_rows[r * heads + h : r * heads + h + 1, :] = queries[
                r : r + 1, h * HEAD : (h + 1) * HEAD
            ]
    len_copy.wait()
    spots = lax.broadcasted_iota(jnp.int32, (per_group, positions), 1)
    for r in range(rows):
        live = spots < lens[r]
        k_copies[r].wait()
        v_copies[r].wait()
        for g in range(KV_HEADS):
            first = r * heads + g * per_group
            q = q_rows[first : first + per_group, :].astype(BF16)
            keys = k_ref[r, :, g * HEAD : (g + 1) * HEAD]
            scores = lax.dot_general(q, keys, NT, preferred_element_type=F32) / math.sqrt(HEAD)
            scores = jnp.where(live, scores, -1e30)
            peak = jnp.max(scores, axis=1, keepdims=True)
            probs = jnp.where(live, jnp.exp(scores - peak), 0.0)
            weight_sum = jnp.sum(probs, axis=1, keepdims=True)
            values = v_ref[r, :, g * HEAD : (g + 1) * HEAD]
            summed = jnp.dot(probs.astype(BF16), values, preferred_element_type=F32)
            summed = summed / weight_sum
            for j in range(per_group):
                h = g * per_group + j
                out_rows[r : r + 1, h * HEAD : (h + 1) * HEAD] = summed[j : j + 1, :]
    out_ref[...] = out_rows[...].astype(BF16)


def attention(lengths, queries, keys, values):
    rows, width = queries.shape
    return pl.pallas_call(
        attention_kernel,
        out_shape=jax.ShapeDtypeStruct((rows, width), BF16),
        in_specs=[ANY] * 4,
        out_specs=VMEM,
        scratch_shapes=[
            pltpu.SMEM(lengths.shape, jnp.int32),
            pltpu.VMEM((rows, width), BF16),
            pltpu.VMEM(keys.shape, BF16),
            pltpu.VMEM(values.shape, BF16),
            pltpu.VMEM((rows * width // HEAD, HEAD), F32),
            pltpu.VMEM((rows, width), F32),
            pltpu.SemaphoreType.DMA((2 + 2 * rows,)),
        ],
        compiler_params=params(16),
        name="attention",
    )(*map(in_hbm, (lengths, queries, keys, values)))


def in_hbm(value):
    return pltpu.with_memory_space_constraint(value, pltpu.HBM)


def fetch_kernel(*refs):
    count = (len(refs) - 2) // 2
    sources, targets, sems = refs[1 : 1 + count], refs[1 + count : -1], refs[-1]
    copies = [
        pltpu.make_async_copy(s, t, sems.at[i]) for i, (s, t) in enumerate(zip(sources, targets))
    ]
    for copy in copies:
        copy.start()
    for copy in copies:
        copy.wait()


def fetch(after, *arrays):
    size = sum(a.size * a.dtype.itemsize for a in arrays)
    return pl.pallas_call(
        fetch_kernel,
        out_shape=[pltpu.VMEM(a.shape, a.dtype) for a in arrays],
        in_specs=[ANY] * (1 + len(arrays)),
        out_specs=[VMEM] * len(arrays),
        scratch_shapes=[pltpu.SemaphoreType.DMA((len(arrays),))],
        compiler_params=params(1),
        cost_estimate=pl.CostEstimate(flops=0, bytes_accessed=size, transcendentals=0),
        name="fetch",
    )(after, *map(in_hbm, arrays))


def routes_of(ids, weights):
    top = ids.shape[0]
    lane = lax.broadcasted_iota(jnp.int32, (ROWS, LANES), 1)
    row = lax.broadcasted_iota(jnp.int32, (ROWS, LANES), 0)
    hi, mid, lo = split3(weights)
    total = jnp.zeros((top, LANES), F32)
    for piece, start in ((ids.astype(F32), IDS), (hi, HI), (mid, MID), (lo, LO)):
        place = (lane == row + start).astype(BF16)
        total += jnp.dot(piece.astype(BF16), place, preferred_element_type=F32)
    return total


def stream_kernel(
    a0, a1, a2, a3, w_ref, residual_ref, gain_ref, ids_ref, weights_ref, stream_ref, unit_ref, rows_ref
):
    part = a0.shape[0]
    for k, a in enumerate((a0, a1, a2, a3)):
        rows_ref[k * part : (k + 1) * part, :] = a[...].astype(F32)
    mixed = jnp.dot(rows_ref[...].astype(BF16), w_ref[...], preferred_element_type=F32)
    half = part // CORES
    z, c = lax.axis_index("z"), lax.axis_index("c")
    here = lax.broadcasted_iota(jnp.int32, (ROWS, ROWS), 1)
    wanted = lax.broadcasted_iota(jnp.int32, (ROWS, ROWS), 0)
    slot, within = here // part, here % part
    owner = (z - slot + SIDE) % SIDE * CORES + (c + within // half) % CORES
    order = (wanted == owner * half + within % half).astype(F32)
    mixed = jnp.dot(order, mixed, precision=lax.Precision.HIGHEST, preferred_element_type=F32)
    stream = (residual_ref[...].astype(F32) + mixed).astype(BF16)
    stream_ref[...] = stream
    widened = stream.astype(F32)
    scaled = (widened * gain_ref[...]).astype(BF16)
    squares = jnp.sum(widened * widened, axis=1, keepdims=True)
    lane = lax.broadcasted_iota(jnp.int32, (ROWS, LANES), 1)
    row = lax.broadcasted_iota(jnp.int32, (ROWS, LANES), 0)
    squares = jnp.sum(jnp.where(lane == row + SQ, squares, 0.0), axis=0, keepdims=True)
    extra = routes_of(ids_ref[...], weights_ref[...])
    line = lax.broadcasted_iota(jnp.int32, extra.shape, 0)
    held = lax.broadcasted_iota(jnp.int32, extra.shape, 1) >= SQ
    for i, piece in enumerate(split3(squares)):
        extra = jnp.where(held & (line == i), piece, extra)
    unit = jnp.concatenate(
        [scaled[:, j * LANES : (j + 1) * LANES] for j in range(CHUNKS)] + [extra.astype(BF16)],
        axis=0,
    )
    for i in range(unit_ref.shape[0]):
        unit_ref[i] = unit


def make_stream(parts, out_proj, residual, gain, ids, weights):
    return pl.pallas_call(
        stream_kernel,
        out_shape=[
            jax.ShapeDtypeStruct((ROWS, COLS), BF16),
            jax.ShapeDtypeStruct((PLACES * SIDE, UNIT + EXTRA, LANES), BF16),
        ],
        in_specs=[VMEM] * 9,
        out_specs=[VMEM, VMEM],
        scratch_shapes=[pltpu.VMEM((ROWS, D), F32)],
        compiler_params=params(4),
        name="stream",
    )(*parts, out_proj, residual, gain, ids, weights)


def column_block(z, c):
    return pl.ds(pl.multiple_of((z * CORES + c) * COLS, COLS), COLS)


def to_columns(lines, start):
    shape = (PLACES, ROWS, LANES)
    lane = lax.broadcasted_iota(jnp.int32, shape, 2)
    row = lax.broadcasted_iota(jnp.int32, shape, 1)
    kept = jnp.where(lane == row + start, jnp.broadcast_to(lines, shape), 0.0)
    return jnp.sum(kept, axis=2, keepdims=True).reshape(PLACES * ROWS, 1)


def down_half(hidden, down_ref, out_ref, c):
    for z in range(SIDE):
        part = jnp.dot(
            hidden, down_ref[:, column_block(z, c)], preferred_element_type=F32
        ).astype(BF16)
        for s in range(PLACES):
            out_ref[s * SIDE + z] = part[s * ROWS : (s + 1) * ROWS]


def experts_kernel(own_ref, other_ref, gate_ref, up_ref, down_ref, hidden_ref, out_ref, x_ref):
    c = lax.axis_index("c")
    local = gate_ref.shape[0] // EXPERT_COLS
    first = (lax.axis_index("x") * SIDE + lax.axis_index("y")) * local
    for s in range(PLACES):
        for z in range(SIDE):
            for half, parity in ((own_ref, c), (other_ref, 1 - c)):
                start = pl.multiple_of((z * CORES + parity) * COLS, COLS)
                for j in range(CHUNKS):
                    x_ref[s * ROWS : (s + 1) * ROWS, pl.ds(start + j * LANES, LANES)] = half[
                        s * SIDE + z, j * ROWS : (j + 1) * ROWS, :
                    ]
    squares = jnp.zeros((PLACES, 1, LANES), F32)
    for s_ref in (own_ref, other_ref):
        extras = s_ref[:, UNIT:, :].astype(F32).reshape(PLACES, SIDE, EXTRA, LANES)
        for z in range(SIDE):
            squares += jnp.sum(extras[:, z, :3, :], axis=1, keepdims=True)
    scale = lax.rsqrt(to_columns(squares, SQ) / D + 1e-06)
    routes = jnp.stack([own_ref[s * SIDE, UNIT:, :] for s in range(PLACES)]).astype(F32)
    weights = (
        pltpu.roll(routes, LANES - HI, 2)
        + pltpu.roll(routes, LANES - MID, 2)
        + pltpu.roll(routes, LANES - LO, 2)
    )
    x = x_ref[...]
    gate = lax.dot_general(x, gate_ref[...], NT, preferred_element_type=F32) * scale
    up = lax.dot_general(x, up_ref[...], NT, preferred_element_type=F32) * scale
    column = lax.broadcasted_iota(jnp.int32, gate.shape, 1)
    mix = None
    for e in range(local):
        mine = jnp.where(routes == (first + e).astype(F32), weights, 0.0)
        one = to_columns(jnp.sum(mine, axis=1, keepdims=True), IDS)
        mix = one if mix is None else jnp.where(column < e * EXPERT_COLS, mix, one)
    hidden = (gate / (1.0 + jnp.exp(-gate)) * up * mix).astype(BF16)
    hidden_ref[...] = hidden
    down_half(hidden, down_ref, out_ref, 1 - c)


def experts(own, other, gate, up, down):
    rows = PLACES * ROWS
    width = gate.shape[0]
    return pl.pallas_call(
        experts_kernel,
        out_shape=[
            jax.ShapeDtypeStruct((rows, width), BF16),
            jax.ShapeDtypeStruct((PLACES * SIDE, ROWS, COLS), BF16),
        ],
        in_specs=[VMEM] * 5,
        out_specs=[VMEM, VMEM],
        scratch_shapes=[pltpu.VMEM((rows, D), BF16)],
        compiler_params=params(20),
        cost_estimate=pl.CostEstimate(
            flops=5 * rows * width * D, bytes_accessed=6 * width * D, transcendentals=rows * width
        ),
        name="experts",
    )(own, other, gate, up, down)


def down_kernel(hidden_ref, down_ref, out_ref):
    down_half(hidden_ref[...], down_ref, out_ref, lax.axis_index("c"))


def down_own(hidden, down):
    rows, width = hidden.shape
    return pl.pallas_call(
        down_kernel,
        out_shape=jax.ShapeDtypeStruct((PLACES * SIDE, ROWS, COLS), BF16),
        in_specs=[VMEM, VMEM],
        out_specs=VMEM,
        compiler_params=params(20),
        cost_estimate=pl.CostEstimate(
            flops=rows * width * D, bytes_accessed=2 * width * D, transcendentals=0
        ),
        name="down_own",
    )(hidden, down)


def exchange(blocks):
    return lax.all_to_all(blocks, ("x", "y", "z"), split_axis=0, concat_axis=0, tiled=True)


def on_device(
    queries,
    key_cache,
    value_cache,
    lengths,
    residual,
    out_proj,
    norm_gain,
    expert_ids,
    route_weights,
    w_gate,
    w_up,
    w_down,
):
    gate = jnp.swapaxes(w_gate, 1, 2).reshape(-1, D)
    up = jnp.swapaxes(w_up, 1, 2).reshape(-1, D)
    down = w_down.reshape(-1, D)
    attended = attention(lengths, queries, key_cache, value_cache)
    pair = jnp.concatenate([attended, swap(attended)], axis=0)
    parts = spread_z(pair)
    out_proj, residual, gain, ids, weights, gate, up = fetch(
        pair, out_proj, residual, norm_gain[None, :], expert_ids.T, route_weights.T, gate, up
    )
    stream, units = make_stream(parts, out_proj, residual, gain, ids, weights)
    own = exchange(units)
    other = swap(own)
    (down,) = fetch(own, down)
    hidden, theirs = experts(own, other, gate, up, down)
    came = swap(theirs)
    mine = down_own(hidden, down)
    total = (mine.astype(F32) + came.astype(F32)).astype(BF16)
    combined = jnp.sum(exchange(total).astype(F32), axis=0)
    return (stream.astype(F32) + combined).astype(BF16)


def solution(mesh):
    devices = mesh.devices.reshape(SIDE, SIDE, SIDE, CORES)
    pool, grp = ("x", "y"), ("z", "c")
    every = pool + grp
    in_specs = (
        P(every, None),
        P(every, None, None),
        P(every, None, None),
        P(every),
        P(pool, grp),
        P(None, grp),
        P(grp),
        P(pool, None),
        P(pool, None),
        P(pool, None, grp),
        P(pool, None, grp),
        P(pool, grp, None),
    )
    return jax.shard_map(
        on_device,
        mesh=Mesh(devices, every),
        in_specs=in_specs,
        out_specs=P(pool, grp),
        check_vma=False,
    )
```

```python
import functools
import math

import jax
import jax.numpy as jnp
from jax import lax
from jax.experimental import pallas as pl
from jax.experimental.pallas import tpu as pltpu
from jax.sharding import Mesh
from jax.sharding import PartitionSpec as P

D = 4096
KV_HEADS = 2
HEAD = 128
LANES = 128
SIDE = 4
CORES = 2
PLACES = SIDE * SIDE
COLS = D // (SIDE * CORES)
CHUNKS = COLS // LANES
ROWS = 16
UNIT = CHUNKS * ROWS
EXTRA = 8
IDS, HI, MID, LO, SQ = 0, ROWS, 2 * ROWS, 3 * ROWS, 4 * ROWS
EXPERT_COLS = 192
F32 = jnp.float32
BF16 = jnp.bfloat16
NT = (((1,), (1,)), ((), ()))
VMEM = pl.BlockSpec(memory_space=pltpu.VMEM)
ANY = pl.BlockSpec(memory_space=pl.ANY)


def params(mib):
    return pltpu.CompilerParams(vmem_limit_bytes=mib * 1024 * 1024)


def split3(value):
    hi = value.astype(BF16).astype(F32)
    mid = (value - hi).astype(BF16).astype(F32)
    lo = value - hi - mid
    return hi, mid, lo


SWAP = [(0, 1), (1, 0)]


def swap(block):
    return lax.ppermute(block, "c", SWAP)


def spread_z(block):
    return [block] + [
        lax.ppermute(block, "z", [(i, (i + k) % SIDE) for i in range(SIDE)])
        for k in range(1, SIDE)
    ]


def attention_kernel(
    len_hbm, q_hbm, k_hbm, v_hbm, w_hbm, out_ref, w_ref, lens, q_ref, k_ref, v_ref, q_rows, out_rows, sems
):
    rows, width = q_ref.shape
    positions = k_ref.shape[1]
    heads = width // HEAD
    per_group = heads // KV_HEADS
    len_copy = pltpu.make_async_copy(len_hbm, lens, sems.at[0])
    q_copy = pltpu.make_async_copy(q_hbm, q_ref, sems.at[1])
    k_copies = [
        pltpu.make_async_copy(k_hbm.at[r], k_ref.at[r], sems.at[2 + r]) for r in range(rows)
    ]
    v_copies = [
        pltpu.make_async_copy(v_hbm.at[r], v_ref.at[r], sems.at[2 + rows + r])
        for r in range(rows)
    ]
    q_copy.start()
    len_copy.start()
    for r in range(rows):
        k_copies[r].start()
        v_copies[r].start()
    w_copy = pltpu.make_async_copy(w_hbm, w_ref, sems.at[2 + 2 * rows])
    w_copy.start()
    q_copy.wait()
    queries = q_ref[...].astype(F32)
    for r in range(rows):
        for h in range(heads):
            q_rows[r * heads + h : r * heads + h + 1, :] = queries[
                r : r + 1, h * HEAD : (h + 1) * HEAD
            ]
    len_copy.wait()
    spots = lax.broadcasted_iota(jnp.int32, (per_group, positions), 1)
    for r in range(rows):
        live = spots < lens[r]
        k_copies[r].wait()
        v_copies[r].wait()
        for g in range(KV_HEADS):
            first = r * heads + g * per_group
            q = q_rows[first : first + per_group, :].astype(BF16)
            keys = k_ref[r, :, g * HEAD : (g + 1) * HEAD]
            scores = lax.dot_general(q, keys, NT, preferred_element_type=F32) / math.sqrt(HEAD)
            scores = jnp.where(live, scores, -1e30)
            peak = jnp.max(scores, axis=1, keepdims=True)
            probs = jnp.where(live, jnp.exp(scores - peak), 0.0)
            weight_sum = jnp.sum(probs, axis=1, keepdims=True)
            values = v_ref[r, :, g * HEAD : (g + 1) * HEAD]
            summed = jnp.dot(probs.astype(BF16), values, preferred_element_type=F32)
            summed = summed / weight_sum
            for j in range(per_group):
                h = g * per_group + j
                out_rows[r : r + 1, h * HEAD : (h + 1) * HEAD] = summed[j : j + 1, :]
    out_ref[...] = out_rows[...].astype(BF16)
    w_copy.wait()


def attention(lengths, queries, keys, values, out_proj):
    rows, width = queries.shape
    return pl.pallas_call(
        attention_kernel,
        out_shape=[jax.ShapeDtypeStruct((rows, width), BF16), pltpu.VMEM(out_proj.shape, BF16)],
        in_specs=[ANY] * 5,
        out_specs=[VMEM] * 2,
        scratch_shapes=[
            pltpu.SMEM(lengths.shape, jnp.int32),
            pltpu.VMEM((rows, width), BF16),
            pltpu.VMEM(keys.shape, BF16),
            pltpu.VMEM(values.shape, BF16),
            pltpu.VMEM((rows * width // HEAD, HEAD), F32),
            pltpu.VMEM((rows, width), F32),
            pltpu.SemaphoreType.DMA((3 + 2 * rows,)),
        ],
        compiler_params=params(16),
        name="attention",
    )(*map(in_hbm, (lengths, queries, keys, values, out_proj)))


def join_kernel(a_ref, b_ref, out_ref):
    rows = a_ref.shape[0]
    out_ref[:rows] = a_ref[...]
    out_ref[rows:] = b_ref[...]


def join(a, b):
    return pl.pallas_call(
        join_kernel,
        out_shape=jax.ShapeDtypeStruct((a.shape[0] + b.shape[0],) + a.shape[1:], a.dtype),
        in_specs=[VMEM] * 2,
        out_specs=VMEM,
        compiler_params=params(1),
        name="join",
    )(a, b)


def in_hbm(value):
    return pltpu.with_memory_space_constraint(value, pltpu.HBM)


def fetch_kernel(*refs):
    count = (len(refs) - 2) // 2
    sources, targets, sems = refs[1 : 1 + count], refs[1 + count : -1], refs[-1]
    copies = [
        pltpu.make_async_copy(s, t, sems.at[i]) for i, (s, t) in enumerate(zip(sources, targets))
    ]
    for copy in copies:
        copy.start()
    for copy in copies:
        copy.wait()


def fetch(after, *arrays):
    size = sum(a.size * a.dtype.itemsize for a in arrays)
    return pl.pallas_call(
        fetch_kernel,
        out_shape=[pltpu.VMEM(a.shape, a.dtype) for a in arrays],
        in_specs=[ANY] * (1 + len(arrays)),
        out_specs=[VMEM] * len(arrays),
        scratch_shapes=[pltpu.SemaphoreType.DMA((len(arrays),))],
        compiler_params=params(1),
        cost_estimate=pl.CostEstimate(flops=0, bytes_accessed=size, transcendentals=0),
        name="fetch",
    )(after, *map(in_hbm, arrays))


def routes_of(ids, weights):
    top = ids.shape[0]
    lane = lax.broadcasted_iota(jnp.int32, (ROWS, LANES), 1)
    row = lax.broadcasted_iota(jnp.int32, (ROWS, LANES), 0)
    hi, mid, lo = split3(weights)
    total = jnp.zeros((top, LANES), F32)
    for piece, start in ((ids.astype(F32), IDS), (hi, HI), (mid, MID), (lo, LO)):
        place = (lane == row + start).astype(BF16)
        total += jnp.dot(piece.astype(BF16), place, preferred_element_type=F32)
    return total


def stream_kernel(
    a0, a1, a2, a3, w_ref, residual_ref, gain_ref, ids_ref, weights_ref, stream_ref, unit_ref, rows_ref
):
    part = a0.shape[0]
    for k, a in enumerate((a0, a1, a2, a3)):
        rows_ref[k * part : (k + 1) * part, :] = a[...].astype(F32)
    mixed = jnp.dot(rows_ref[...].astype(BF16), w_ref[...], preferred_element_type=F32)
    half = part // CORES
    z, c = lax.axis_index("z"), lax.axis_index("c")
    here = lax.broadcasted_iota(jnp.int32, (ROWS, ROWS), 1)
    wanted = lax.broadcasted_iota(jnp.int32, (ROWS, ROWS), 0)
    slot, within = here // part, here % part
    owner = (z - slot + SIDE) % SIDE * CORES + (c + within // half) % CORES
    order = (wanted == owner * half + within % half).astype(F32)
    mixed = jnp.dot(order, mixed, precision=lax.Precision.HIGHEST, preferred_element_type=F32)
    stream = (residual_ref[...].astype(F32) + mixed).astype(BF16)
    stream_ref[...] = stream
    widened = stream.astype(F32)
    scaled = (widened * gain_ref[...]).astype(BF16)
    squares = jnp.sum(widened * widened, axis=1, keepdims=True)
    lane = lax.broadcasted_iota(jnp.int32, (ROWS, LANES), 1)
    row = lax.broadcasted_iota(jnp.int32, (ROWS, LANES), 0)
    squares = jnp.sum(jnp.where(lane == row + SQ, squares, 0.0), axis=0, keepdims=True)
    extra = routes_of(ids_ref[...], weights_ref[...])
    line = lax.broadcasted_iota(jnp.int32, extra.shape, 0)
    held = lax.broadcasted_iota(jnp.int32, extra.shape, 1) >= SQ
    for i, piece in enumerate(split3(squares)):
        extra = jnp.where(held & (line == i), piece, extra)
    unit = jnp.concatenate(
        [scaled[:, j * LANES : (j + 1) * LANES] for j in range(CHUNKS)] + [extra.astype(BF16)],
        axis=0,
    )
    for i in range(unit_ref.shape[0]):
        unit_ref[i] = unit


def make_stream(parts, out_proj, residual, gain, ids, weights):
    return pl.pallas_call(
        stream_kernel,
        out_shape=[
            jax.ShapeDtypeStruct((ROWS, COLS), BF16),
            jax.ShapeDtypeStruct((PLACES * SIDE, UNIT + EXTRA, LANES), BF16),
        ],
        in_specs=[VMEM] * 9,
        out_specs=[VMEM, VMEM],
        scratch_shapes=[pltpu.VMEM((ROWS, D), F32)],
        compiler_params=params(4),
        name="stream",
    )(*parts, out_proj, residual, gain, ids, weights)


def to_columns(lines, start):
    shape = (PLACES, ROWS, LANES)
    lane = lax.broadcasted_iota(jnp.int32, shape, 2)
    row = lax.broadcasted_iota(jnp.int32, shape, 1)
    kept = jnp.where(lane == row + start, jnp.broadcast_to(lines, shape), 0.0)
    return jnp.sum(kept, axis=2, keepdims=True).reshape(PLACES * ROWS, 1)


def gather_rows(units_ref, x_ref):
    for s in range(PLACES):
        for z in range(SIDE):
            for j in range(CHUNKS):
                start = z * COLS + j * LANES
                x_ref[s * ROWS : (s + 1) * ROWS, start : start + LANES] = units_ref[
                    s * SIDE + z, j * ROWS : (j + 1) * ROWS, :
                ]


def columns_of(z, parity):
    return pl.ds(pl.multiple_of((z * CORES + parity) * COLS, COLS), COLS)


def products(x_ref, w_ref, parity, first=0, count=None):
    count = count or w_ref.shape[0]
    total = None
    for z in range(SIDE):
        part = lax.dot_general(
            x_ref[:, z * COLS : (z + 1) * COLS],
            w_ref[first : first + count, columns_of(z, parity)],
            NT,
            preferred_element_type=F32,
        )
        total = part if total is None else total + part
    return total


def squares_of(units):
    extras = units[:, UNIT : UNIT + 3, :].astype(F32)
    extras = jnp.sum(extras, axis=1, keepdims=True).reshape(PLACES, SIDE, 1, LANES)
    return sum(extras[:, z] for z in range(SIDE))


def own_kernel(own_ref, gate_ref, up_ref, down_ref, gate_sum, up_sum, mix_ref, squares_ref, x_ref):
    c = lax.axis_index("c")
    gather_rows(own_ref, x_ref)
    squares_ref[...] = squares_of(own_ref)
    routes = jnp.stack([own_ref[s * SIDE, UNIT:, :] for s in range(PLACES)]).astype(F32)
    weights = (
        pltpu.roll(routes, LANES - HI, 2)
        + pltpu.roll(routes, LANES - MID, 2)
        + pltpu.roll(routes, LANES - LO, 2)
    )
    local = gate_ref.shape[0] // EXPERT_COLS
    first = (lax.axis_index("x") * SIDE + lax.axis_index("y")) * local
    column = lax.broadcasted_iota(jnp.int32, mix_ref.shape, 1)
    mix = None
    for e in range(local):
        mine = jnp.where(routes == (first + e).astype(F32), weights, 0.0)
        one = to_columns(jnp.sum(mine, axis=1, keepdims=True), IDS)
        mix = one if mix is None else jnp.where(column < e * EXPERT_COLS, mix, one)
    mix_ref[...] = mix
    gate_sum[...] = products(x_ref, gate_ref, c)
    up_sum[...] = products(x_ref, up_ref, c)


def own_part(own, gate, up, down):
    rows = PLACES * ROWS
    width = gate.shape[0]
    return pl.pallas_call(
        own_kernel,
        out_shape=[jax.ShapeDtypeStruct((rows, width), F32)] * 3
        + [jax.ShapeDtypeStruct((PLACES, 1, LANES), F32)],
        in_specs=[VMEM] * 4,
        out_specs=[VMEM] * 4,
        scratch_shapes=[pltpu.VMEM((rows, D // CORES), BF16)],
        compiler_params=params(8),
        name="own_part",
    )(own, gate, up, down)


PARTS = 3


def hidden_kernel(
    other_ref, gate_ref, up_ref, gate_in, up_in, mix_ref, squares_ref, down_ref, hidden_ref, out_ref, x_ref
):
    other = 1 - lax.axis_index("c")
    gather_rows(other_ref, x_ref)
    scale = lax.rsqrt(to_columns(squares_ref[...] + squares_of(other_ref), SQ) / D + 1e-06)
    width = hidden_ref.shape[1] // PARTS
    for i in range(PARTS):
        first = i * width
        part = slice(first, first + width)
        half = (gate_in[:, part] + products(x_ref, gate_ref, other, first, width)) * (0.5 * scale)
        up = (up_in[:, part] + products(x_ref, up_ref, other, first, width)) * scale
        hidden_ref[:, part] = ((half + half * jnp.tanh(half)) * up * mix_ref[:, part]).astype(BF16)
    down_part(hidden_ref, down_ref, other, out_ref, 0)


def down_part(hidden_ref, down_ref, parity, out_ref, first):
    for z in range(out_ref.shape[1]):
        part = jnp.dot(
            hidden_ref[...],
            down_ref[:, columns_of(first + z, parity)],
            preferred_element_type=F32,
        ).astype(BF16)
        for s in range(PLACES):
            out_ref[s, z] = part[s * ROWS : (s + 1) * ROWS]


HALF = SIDE // 2


def blocks(count):
    return jax.ShapeDtypeStruct((PLACES, count, ROWS, COLS), BF16)


def make_hidden(other, gate, up, sums, down):
    rows = PLACES * ROWS
    width = gate.shape[0]
    return pl.pallas_call(
        hidden_kernel,
        out_shape=[jax.ShapeDtypeStruct((rows, width), BF16), blocks(HALF)],
        in_specs=[VMEM] * 8,
        out_specs=[VMEM] * 2,
        scratch_shapes=[pltpu.VMEM((rows, D // CORES), BF16)],
        compiler_params=params(12),
        name="hidden",
    )(other, gate, up, *sums, down)


def down_kernel(mine, hidden_ref, down_ref, out_ref):
    c = lax.axis_index("c")
    if mine:
        down_part(hidden_ref, down_ref, c, out_ref, 0)
    else:
        down_part(hidden_ref, down_ref, 1 - c, out_ref, HALF)


def down_blocks(mine, hidden, down):
    count = SIDE if mine else HALF
    return pl.pallas_call(
        functools.partial(down_kernel, mine),
        out_shape=blocks(count),
        in_specs=[VMEM, VMEM],
        out_specs=VMEM,
        compiler_params=params(4),
        cost_estimate=pl.CostEstimate(flops=1, bytes_accessed=1, transcendentals=0),
        name="down_mine" if mine else "down_theirs",
    )(hidden, down)


def add_kernel(mine_ref, first_ref, second_ref, out_ref):
    for i, came_ref in enumerate((first_ref, second_ref)):
        zs = slice(i * HALF, (i + 1) * HALF)
        total = mine_ref[:, zs].astype(F32) + came_ref[...].astype(F32)
        out_ref[:, zs] = total.astype(BF16)


def add(mine, first, second):
    return pl.pallas_call(
        add_kernel,
        out_shape=blocks(SIDE),
        in_specs=[VMEM] * 3,
        out_specs=VMEM,
        compiler_params=params(4),
        name="add",
    )(mine, first, second)


def finish_kernel(parts_ref, stream_ref, out_hbm, out_ref, sem):
    total = stream_ref[...].astype(F32)
    for i in range(parts_ref.shape[0]):
        total += parts_ref[i].astype(F32)
    out_ref[...] = total.astype(BF16)
    copy = pltpu.make_async_copy(out_ref, out_hbm, sem)
    copy.start()
    copy.wait()


def finish(parts, stream):
    return pl.pallas_call(
        finish_kernel,
        out_shape=jax.ShapeDtypeStruct(stream.shape, BF16),
        in_specs=[VMEM] * 2,
        out_specs=ANY,
        scratch_shapes=[pltpu.VMEM(stream.shape, BF16), pltpu.SemaphoreType.DMA],
        compiler_params=params(4),
        name="finish",
    )(parts, stream)


def exchange(blocks):
    return lax.all_to_all(blocks, ("x", "y", "z"), split_axis=0, concat_axis=0, tiled=True)


def on_device(
    queries,
    key_cache,
    value_cache,
    lengths,
    residual,
    out_proj,
    norm_gain,
    expert_ids,
    route_weights,
    w_gate,
    w_up,
    w_down,
):
    gate = jnp.swapaxes(w_gate, 1, 2).reshape(-1, D)
    up = jnp.swapaxes(w_up, 1, 2).reshape(-1, D)
    down = w_down.reshape(-1, D)
    attended, out_proj = attention(lengths, queries, key_cache, value_cache, out_proj)
    pair = join(attended, swap(attended))
    parts = spread_z(pair)
    residual, gain, ids, weights, gate = fetch(
        pair, residual, norm_gain[None, :], expert_ids.T, route_weights.T, gate
    )
    stream, units = make_stream(parts, out_proj, residual, gain, ids, weights)
    own = exchange(units)
    other = swap(own)
    sums = own_part(own, gate, up, down)
    hidden, theirs = make_hidden(other, gate, up, sums, down)
    first = swap(theirs)
    second = swap(down_blocks(False, hidden, down))
    mine = down_blocks(True, hidden, down)
    total = add(mine, first, second).reshape(PLACES * SIDE, ROWS, COLS)
    return finish(exchange(total), stream)


def solution(mesh):
    devices = mesh.devices.reshape(SIDE, SIDE, SIDE, CORES)
    pool, grp = ("x", "y"), ("z", "c")
    every = pool + grp
    in_specs = (
        P(every, None),
        P(every, None, None),
        P(every, None, None),
        P(every),
        P(pool, grp),
        P(None, grp),
        P(grp),
        P(pool, None),
        P(pool, None),
        P(pool, None, grp),
        P(pool, None, grp),
        P(pool, grp, None),
    )
    return jax.shard_map(
        on_device,
        mesh=Mesh(devices, every),
        in_specs=in_specs,
        out_specs=P(pool, grp),
        check_vma=False,
    )
```

```python
import functools
import math
import random

import jax
import jax.numpy as jnp
from jax import lax
from jax.experimental import pallas as pl
from jax.experimental.pallas import tpu as pltpu
from jax.sharding import Mesh
from jax.sharding import PartitionSpec as P

D = 4096
KV_HEADS = 2
HEAD = 128
LANES = 128
SIDE = 4
CORES = 2
PLACES = SIDE * SIDE
COLS = D // (SIDE * CORES)
CHUNKS = COLS // LANES
ROWS = 16
UNIT = CHUNKS * ROWS
EXTRA = 8
IDS, HI, MID, LO, SQ = 0, ROWS, 2 * ROWS, 3 * ROWS, 4 * ROWS
EXPERT_COLS = 192
ORDER = list(range(PLACES * SIDE))
random.Random(1).shuffle(ORDER)
RANK = [ORDER.index(place) for place in range(PLACES * SIDE)]
GROUPS = [[place * CORES + c for place in ORDER] for c in range(CORES)]
F32 = jnp.float32
BF16 = jnp.bfloat16
NT = (((1,), (1,)), ((), ()))
VMEM = pl.BlockSpec(memory_space=pltpu.VMEM)
ANY = pl.BlockSpec(memory_space=pl.ANY)


def params(mib):
    return pltpu.CompilerParams(vmem_limit_bytes=mib * 1024 * 1024)


def split3(value):
    hi = value.astype(BF16).astype(F32)
    mid = (value - hi).astype(BF16).astype(F32)
    lo = value - hi - mid
    return hi, mid, lo


SWAP = [(0, 1), (1, 0)]


def swap(block):
    return lax.ppermute(block, "c", SWAP)


def spread_z(block):
    return [block] + [
        lax.ppermute(block, "z", [(i, (i + k) % SIDE) for i in range(SIDE)])
        for k in range(1, SIDE)
    ]


def attention_kernel(
    len_hbm, q_hbm, k_hbm, v_hbm, w_hbm, out_ref, w_ref, lens, q_ref, k_ref, v_ref, q_rows, out_rows, sems
):
    rows, width = q_ref.shape
    positions = k_ref.shape[1]
    heads = width // HEAD
    per_group = heads // KV_HEADS
    len_copy = pltpu.make_async_copy(len_hbm, lens, sems.at[0])
    q_copy = pltpu.make_async_copy(q_hbm, q_ref, sems.at[1])
    k_copies = [
        pltpu.make_async_copy(k_hbm.at[r], k_ref.at[r], sems.at[2 + r]) for r in range(rows)
    ]
    v_copies = [
        pltpu.make_async_copy(v_hbm.at[r], v_ref.at[r], sems.at[2 + rows + r])
        for r in range(rows)
    ]
    q_copy.start()
    len_copy.start()
    for r in range(rows):
        k_copies[r].start()
        v_copies[r].start()
    w_copy = pltpu.make_async_copy(w_hbm, w_ref, sems.at[2 + 2 * rows])
    w_copy.start()
    q_copy.wait()
    queries = q_ref[...].astype(F32)
    for r in range(rows):
        for h in range(heads):
            q_rows[r * heads + h : r * heads + h + 1, :] = queries[
                r : r + 1, h * HEAD : (h + 1) * HEAD
            ]
    len_copy.wait()
    spots = lax.broadcasted_iota(jnp.int32, (per_group, positions), 1)
    for r in range(rows):
        live = spots < lens[r]
        k_copies[r].wait()
        v_copies[r].wait()
        for g in range(KV_HEADS):
            first = r * heads + g * per_group
            q = q_rows[first : first + per_group, :].astype(BF16)
            keys = k_ref[r, :, g * HEAD : (g + 1) * HEAD]
            scores = lax.dot_general(q, keys, NT, preferred_element_type=F32) / math.sqrt(HEAD)
            scores = jnp.where(live, scores, -1e30)
            peak = jnp.max(scores, axis=1, keepdims=True)
            probs = jnp.where(live, jnp.exp(scores - peak), 0.0)
            weight_sum = jnp.sum(probs, axis=1, keepdims=True)
            values = v_ref[r, :, g * HEAD : (g + 1) * HEAD]
            summed = jnp.dot(probs.astype(BF16), values, preferred_element_type=F32)
            summed = summed / weight_sum
            for j in range(per_group):
                h = g * per_group + j
                out_rows[r : r + 1, h * HEAD : (h + 1) * HEAD] = summed[j : j + 1, :]
    out_ref[...] = out_rows[...].astype(BF16)
    w_copy.wait()


def attention(lengths, queries, keys, values, out_proj):
    rows, width = queries.shape
    return pl.pallas_call(
        attention_kernel,
        out_shape=[jax.ShapeDtypeStruct((rows, width), BF16), pltpu.VMEM(out_proj.shape, BF16)],
        in_specs=[ANY] * 5,
        out_specs=[VMEM] * 2,
        scratch_shapes=[
            pltpu.SMEM(lengths.shape, jnp.int32),
            pltpu.VMEM((rows, width), BF16),
            pltpu.VMEM(keys.shape, BF16),
            pltpu.VMEM(values.shape, BF16),
            pltpu.VMEM((rows * width // HEAD, HEAD), F32),
            pltpu.VMEM((rows, width), F32),
            pltpu.SemaphoreType.DMA((3 + 2 * rows,)),
        ],
        compiler_params=params(16),
        name="attention",
    )(*map(in_hbm, (lengths, queries, keys, values, out_proj)))


def join_kernel(a_ref, b_ref, out_ref):
    rows = a_ref.shape[0]
    out_ref[:rows] = a_ref[...]
    out_ref[rows:] = b_ref[...]


def join(a, b):
    return pl.pallas_call(
        join_kernel,
        out_shape=jax.ShapeDtypeStruct((a.shape[0] + b.shape[0],) + a.shape[1:], a.dtype),
        in_specs=[VMEM] * 2,
        out_specs=VMEM,
        compiler_params=params(1),
        name="join",
    )(a, b)


def in_hbm(value):
    return pltpu.with_memory_space_constraint(value, pltpu.HBM)


def fetch_kernel(*refs):
    count = (len(refs) - 2) // 2
    sources, targets, sems = refs[1 : 1 + count], refs[1 + count : -1], refs[-1]
    copies = [
        pltpu.make_async_copy(s, t, sems.at[i]) for i, (s, t) in enumerate(zip(sources, targets))
    ]
    for copy in copies:
        copy.start()
    for copy in copies:
        copy.wait()


def fetch(after, *arrays):
    size = sum(a.size * a.dtype.itemsize for a in arrays)
    return pl.pallas_call(
        fetch_kernel,
        out_shape=[pltpu.VMEM(a.shape, a.dtype) for a in arrays],
        in_specs=[ANY] * (1 + len(arrays)),
        out_specs=[VMEM] * len(arrays),
        scratch_shapes=[pltpu.SemaphoreType.DMA((len(arrays),))],
        compiler_params=params(1),
        cost_estimate=pl.CostEstimate(flops=0, bytes_accessed=size, transcendentals=0),
        name="fetch",
    )(after, *map(in_hbm, arrays))


def routes_of(ids, weights):
    top = ids.shape[0]
    lane = lax.broadcasted_iota(jnp.int32, (ROWS, LANES), 1)
    row = lax.broadcasted_iota(jnp.int32, (ROWS, LANES), 0)
    hi, mid, lo = split3(weights)
    total = jnp.zeros((top, LANES), F32)
    for piece, start in ((ids.astype(F32), IDS), (hi, HI), (mid, MID), (lo, LO)):
        place = (lane == row + start).astype(BF16)
        total += jnp.dot(piece.astype(BF16), place, preferred_element_type=F32)
    return total


def stream_kernel(
    a0, a1, a2, a3, w_ref, residual_ref, gain_ref, ids_ref, weights_ref, stream_ref, unit_ref, rows_ref
):
    part = a0.shape[0]
    for k, a in enumerate((a0, a1, a2, a3)):
        rows_ref[k * part : (k + 1) * part, :] = a[...].astype(F32)
    mixed = jnp.dot(rows_ref[...].astype(BF16), w_ref[...], preferred_element_type=F32)
    half = part // CORES
    z, c = lax.axis_index("z"), lax.axis_index("c")
    here = lax.broadcasted_iota(jnp.int32, (ROWS, ROWS), 1)
    wanted = lax.broadcasted_iota(jnp.int32, (ROWS, ROWS), 0)
    slot, within = here // part, here % part
    owner = (z - slot + SIDE) % SIDE * CORES + (c + within // half) % CORES
    order = (wanted == owner * half + within % half).astype(F32)
    mixed = jnp.dot(order, mixed, precision=lax.Precision.HIGHEST, preferred_element_type=F32)
    stream = (residual_ref[...].astype(F32) + mixed).astype(BF16)
    stream_ref[...] = stream
    widened = stream.astype(F32)
    scaled = (widened * gain_ref[...]).astype(BF16)
    squares = jnp.sum(widened * widened, axis=1, keepdims=True)
    lane = lax.broadcasted_iota(jnp.int32, (ROWS, LANES), 1)
    row = lax.broadcasted_iota(jnp.int32, (ROWS, LANES), 0)
    squares = jnp.sum(jnp.where(lane == row + SQ, squares, 0.0), axis=0, keepdims=True)
    extra = routes_of(ids_ref[...], weights_ref[...])
    line = lax.broadcasted_iota(jnp.int32, extra.shape, 0)
    held = lax.broadcasted_iota(jnp.int32, extra.shape, 1) >= SQ
    for i, piece in enumerate(split3(squares)):
        extra = jnp.where(held & (line == i), piece, extra)
    unit = jnp.concatenate(
        [scaled[:, j * LANES : (j + 1) * LANES] for j in range(CHUNKS)] + [extra.astype(BF16)],
        axis=0,
    )
    for i in range(unit_ref.shape[0]):
        unit_ref[i] = unit


def make_stream(parts, out_proj, residual, gain, ids, weights):
    return pl.pallas_call(
        stream_kernel,
        out_shape=[
            jax.ShapeDtypeStruct((ROWS, COLS), BF16),
            jax.ShapeDtypeStruct((PLACES * SIDE, UNIT + EXTRA, LANES), BF16),
        ],
        in_specs=[VMEM] * 9,
        out_specs=[VMEM, VMEM],
        scratch_shapes=[pltpu.VMEM((ROWS, D), F32)],
        compiler_params=params(4),
        name="stream",
    )(*parts, out_proj, residual, gain, ids, weights)


def to_columns(lines, start):
    shape = (PLACES, ROWS, LANES)
    lane = lax.broadcasted_iota(jnp.int32, shape, 2)
    row = lax.broadcasted_iota(jnp.int32, shape, 1)
    kept = jnp.where(lane == row + start, jnp.broadcast_to(lines, shape), 0.0)
    return jnp.sum(kept, axis=2, keepdims=True).reshape(PLACES * ROWS, 1)


def gather_rows(units_ref, x_ref):
    for s in range(PLACES):
        for z in range(SIDE):
            for j in range(CHUNKS):
                start = z * COLS + j * LANES
                x_ref[s * ROWS : (s + 1) * ROWS, start : start + LANES] = units_ref[
                    RANK[s * SIDE + z], j * ROWS : (j + 1) * ROWS, :
                ]


def columns_of(z, parity):
    return pl.ds(pl.multiple_of((z * CORES + parity) * COLS, COLS), COLS)


def products(x_ref, w_ref, parity, first=0, count=None):
    count = count or w_ref.shape[0]
    total = None
    for z in range(SIDE):
        part = lax.dot_general(
            x_ref[:, z * COLS : (z + 1) * COLS],
            w_ref[first : first + count, columns_of(z, parity)],
            NT,
            preferred_element_type=F32,
        )
        total = part if total is None else total + part
    return total


def squares_of(units):
    extras = jnp.sum(units[:, UNIT : UNIT + 3, :].astype(F32), axis=1, keepdims=True)
    return sum(
        jnp.stack([extras[RANK[s * SIDE + z]] for s in range(PLACES)]) for z in range(SIDE)
    )


def own_kernel(own_ref, gate_ref, up_ref, down_ref, gate_sum, up_sum, mix_ref, squares_ref, x_ref):
    c = lax.axis_index("c")
    gather_rows(own_ref, x_ref)
    squares_ref[...] = squares_of(own_ref)
    routes = jnp.stack([own_ref[RANK[s * SIDE], UNIT:, :] for s in range(PLACES)]).astype(F32)
    weights = (
        pltpu.roll(routes, LANES - HI, 2)
        + pltpu.roll(routes, LANES - MID, 2)
        + pltpu.roll(routes, LANES - LO, 2)
    )
    local = gate_ref.shape[0] // EXPERT_COLS
    first = (lax.axis_index("x") * SIDE + lax.axis_index("y")) * local
    column = lax.broadcasted_iota(jnp.int32, mix_ref.shape, 1)
    mix = None
    for e in range(local):
        mine = jnp.where(routes == (first + e).astype(F32), weights, 0.0)
        one = to_columns(jnp.sum(mine, axis=1, keepdims=True), IDS)
        mix = one if mix is None else jnp.where(column < e * EXPERT_COLS, mix, one)
    mix_ref[...] = mix
    gate_sum[...] = products(x_ref, gate_ref, c)
    up_sum[...] = products(x_ref, up_ref, c)


def own_part(own, gate, up, down):
    rows = PLACES * ROWS
    width = gate.shape[0]
    return pl.pallas_call(
        own_kernel,
        out_shape=[jax.ShapeDtypeStruct((rows, width), F32)] * 3
        + [jax.ShapeDtypeStruct((PLACES, 1, LANES), F32)],
        in_specs=[VMEM] * 4,
        out_specs=[VMEM] * 4,
        scratch_shapes=[pltpu.VMEM((rows, D // CORES), BF16)],
        compiler_params=params(8),
        name="own_part",
    )(own, gate, up, down)


PARTS = 3


def hidden_kernel(
    other_ref, gate_ref, up_ref, gate_in, up_in, mix_ref, squares_ref, down_ref, hidden_ref, out_ref, x_ref
):
    other = 1 - lax.axis_index("c")
    gather_rows(other_ref, x_ref)
    scale = lax.rsqrt(to_columns(squares_ref[...] + squares_of(other_ref), SQ) / D + 1e-06)
    width = hidden_ref.shape[1] // PARTS
    for i in range(PARTS):
        first = i * width
        part = slice(first, first + width)
        half = (gate_in[:, part] + products(x_ref, gate_ref, other, first, width)) * (0.5 * scale)
        up = (up_in[:, part] + products(x_ref, up_ref, other, first, width)) * scale
        hidden_ref[:, part] = ((half + half * jnp.tanh(half)) * up * mix_ref[:, part]).astype(BF16)
    down_part(hidden_ref, down_ref, other, out_ref, 0)


def down_part(hidden_ref, down_ref, parity, out_ref, first):
    for z in range(out_ref.shape[1]):
        part = jnp.dot(
            hidden_ref[...],
            down_ref[:, columns_of(first + z, parity)],
            preferred_element_type=F32,
        ).astype(BF16)
        for s in range(PLACES):
            out_ref[s, z] = part[s * ROWS : (s + 1) * ROWS]


HALF = SIDE // 2


def blocks(count):
    return jax.ShapeDtypeStruct((PLACES, count, ROWS, COLS), BF16)


def make_hidden(other, gate, up, sums, down):
    rows = PLACES * ROWS
    width = gate.shape[0]
    return pl.pallas_call(
        hidden_kernel,
        out_shape=[jax.ShapeDtypeStruct((rows, width), BF16), blocks(HALF)],
        in_specs=[VMEM] * 8,
        out_specs=[VMEM] * 2,
        scratch_shapes=[pltpu.VMEM((rows, D // CORES), BF16)],
        compiler_params=params(12),
        name="hidden",
    )(other, gate, up, *sums, down)


def down_kernel(mine, hidden_ref, down_ref, out_ref):
    c = lax.axis_index("c")
    if mine:
        down_part(hidden_ref, down_ref, c, out_ref, 0)
    else:
        down_part(hidden_ref, down_ref, 1 - c, out_ref, HALF)


def down_blocks(mine, hidden, down):
    count = SIDE if mine else HALF
    return pl.pallas_call(
        functools.partial(down_kernel, mine),
        out_shape=blocks(count),
        in_specs=[VMEM, VMEM],
        out_specs=VMEM,
        compiler_params=params(4),
        cost_estimate=pl.CostEstimate(flops=1, bytes_accessed=1, transcendentals=0),
        name="down_mine" if mine else "down_theirs",
    )(hidden, down)


def add_kernel(mine_ref, first_ref, second_ref, out_ref):
    for i, came_ref in enumerate((first_ref, second_ref)):
        for z in range(HALF):
            total = mine_ref[:, i * HALF + z].astype(F32) + came_ref[:, z].astype(F32)
            for s in range(PLACES):
                out_ref[RANK[s * SIDE + i * HALF + z]] = total[s].astype(BF16)


def add(mine, first, second):
    return pl.pallas_call(
        add_kernel,
        out_shape=jax.ShapeDtypeStruct((PLACES * SIDE, ROWS, COLS), BF16),
        in_specs=[VMEM] * 3,
        out_specs=VMEM,
        compiler_params=params(4),
        name="add",
    )(mine, first, second)


def finish_kernel(parts_ref, stream_ref, out_hbm, out_ref, sem):
    total = stream_ref[...].astype(F32)
    for i in range(parts_ref.shape[0]):
        total += parts_ref[i].astype(F32)
    out_ref[...] = total.astype(BF16)
    copy = pltpu.make_async_copy(out_ref, out_hbm, sem)
    copy.start()
    copy.wait()


def finish(parts, stream):
    return pl.pallas_call(
        finish_kernel,
        out_shape=jax.ShapeDtypeStruct(stream.shape, BF16),
        in_specs=[VMEM] * 2,
        out_specs=ANY,
        scratch_shapes=[pltpu.VMEM(stream.shape, BF16), pltpu.SemaphoreType.DMA],
        compiler_params=params(4),
        name="finish",
    )(parts, stream)


def exchange(blocks):
    axes = ("x", "y", "z", "c")
    return lax.all_to_all(
        blocks, axes, split_axis=0, concat_axis=0, axis_index_groups=GROUPS, tiled=True
    )


def on_device(
    queries,
    key_cache,
    value_cache,
    lengths,
    residual,
    out_proj,
    norm_gain,
    expert_ids,
    route_weights,
    w_gate,
    w_up,
    w_down,
):
    gate = jnp.swapaxes(w_gate, 1, 2).reshape(-1, D)
    up = jnp.swapaxes(w_up, 1, 2).reshape(-1, D)
    down = w_down.reshape(-1, D)
    attended, out_proj = attention(lengths, queries, key_cache, value_cache, out_proj)
    pair = join(attended, swap(attended))
    parts = spread_z(pair)
    residual, gain, ids, weights, gate = fetch(
        pair, residual, norm_gain[None, :], expert_ids.T, route_weights.T, gate
    )
    stream, units = make_stream(parts, out_proj, residual, gain, ids, weights)
    own = exchange(units)
    other = swap(own)
    sums = own_part(own, gate, up, down)
    hidden, theirs = make_hidden(other, gate, up, sums, down)
    first = swap(theirs)
    second = swap(down_blocks(False, hidden, down))
    mine = down_blocks(True, hidden, down)
    return finish(exchange(add(mine, first, second)), stream)


def solution(mesh):
    devices = mesh.devices.reshape(SIDE, SIDE, SIDE, CORES)
    pool, grp = ("x", "y"), ("z", "c")
    every = pool + grp
    in_specs = (
        P(every, None),
        P(every, None, None),
        P(every, None, None),
        P(every),
        P(pool, grp),
        P(None, grp),
        P(grp),
        P(pool, None),
        P(pool, None),
        P(pool, None, grp),
        P(pool, None, grp),
        P(pool, grp, None),
    )
    return jax.shard_map(
        on_device,
        mesh=Mesh(devices, every),
        in_specs=in_specs,
        out_specs=P(pool, grp),
        check_vma=False,
    )
```

```python
import functools
import math
import random

import jax
import jax.numpy as jnp
from jax import lax
from jax.experimental import pallas as pl
from jax.experimental.pallas import tpu as pltpu
from jax.sharding import Mesh
from jax.sharding import PartitionSpec as P

D = 4096
KV_HEADS = 2
HEAD = 128
LANES = 128
SIDE = 4
CORES = 2
PLACES = SIDE * SIDE
COLS = D // (SIDE * CORES)
CHUNKS = COLS // LANES
ROWS = 16
UNIT = CHUNKS * ROWS
EXTRA = 8
IDS, HI, MID, LO, SQ = 0, ROWS, 2 * ROWS, 3 * ROWS, 4 * ROWS
EXPERT_COLS = 192
ORDER = list(range(PLACES * SIDE))
random.Random(1).shuffle(ORDER)
RANK = [ORDER.index(place) for place in range(PLACES * SIDE)]
GROUPS = [[place * CORES + c for place in ORDER] for c in range(CORES)]
F32 = jnp.float32
BF16 = jnp.bfloat16
NT = (((1,), (1,)), ((), ()))
VMEM = pl.BlockSpec(memory_space=pltpu.VMEM)
ANY = pl.BlockSpec(memory_space=pl.ANY)


def params(mib):
    return pltpu.CompilerParams(vmem_limit_bytes=mib * 1024 * 1024)


def split3(value):
    hi = value.astype(BF16).astype(F32)
    mid = (value - hi).astype(BF16).astype(F32)
    lo = value - hi - mid
    return hi, mid, lo


SWAP = [(0, 1), (1, 0)]


def swap(block):
    return lax.ppermute(block, "c", SWAP)


def spread_z(block):
    return [block] + [
        lax.ppermute(block, "z", [(i, (i + k) % SIDE) for i in range(SIDE)])
        for k in range(1, SIDE)
    ]


def attention_kernel(
    len_hbm, q_hbm, k_hbm, v_hbm, out_ref, lens, q_ref, k_ref, v_ref, q_rows, out_rows, sems
):
    rows, width = q_ref.shape
    positions = k_ref.shape[1]
    heads = width // HEAD
    per_group = heads // KV_HEADS
    len_copy = pltpu.make_async_copy(len_hbm, lens, sems.at[0])
    q_copy = pltpu.make_async_copy(q_hbm, q_ref, sems.at[1])
    k_copies = [
        pltpu.make_async_copy(k_hbm.at[r], k_ref.at[r], sems.at[2 + r]) for r in range(rows)
    ]
    v_copies = [
        pltpu.make_async_copy(v_hbm.at[r], v_ref.at[r], sems.at[2 + rows + r])
        for r in range(rows)
    ]
    q_copy.start()
    len_copy.start()
    for copy in k_copies + v_copies:
        copy.start()
    q_copy.wait()
    queries = q_ref[...].astype(F32)
    for r in range(rows):
        for h in range(heads):
            q_rows[r * heads + h : r * heads + h + 1, :] = queries[
                r : r + 1, h * HEAD : (h + 1) * HEAD
            ]
    len_copy.wait()
    spots = lax.broadcasted_iota(jnp.int32, (per_group, positions), 1)
    cases = [(r, g) for r in range(rows) for g in range(KV_HEADS)]
    for copy in k_copies:
        copy.wait()
    scores = []
    for r, g in cases:
        first = r * heads + g * per_group
        q = q_rows[first : first + per_group, :].astype(BF16)
        keys = k_ref[r, :, g * HEAD : (g + 1) * HEAD]
        product = lax.dot_general(q, keys, NT, preferred_element_type=F32) / math.sqrt(HEAD)
        scores.append(jnp.where(spots < lens[r], product, -1e30))
    peaks = [jnp.max(x, axis=1, keepdims=True) for x in scores]
    probs = [
        jnp.where(spots < lens[r], jnp.exp(x - peak), 0.0)
        for (r, g), x, peak in zip(cases, scores, peaks)
    ]
    sums = [jnp.sum(x, axis=1, keepdims=True) for x in probs]
    for copy in v_copies:
        copy.wait()
    for (r, g), x, weight_sum in zip(cases, probs, sums):
        values = v_ref[r, :, g * HEAD : (g + 1) * HEAD]
        summed = jnp.dot(x.astype(BF16), values, preferred_element_type=F32) / weight_sum
        for j in range(per_group):
            h = g * per_group + j
            out_rows[r : r + 1, h * HEAD : (h + 1) * HEAD] = summed[j : j + 1, :]
    out_ref[...] = out_rows[...].astype(BF16)


def attention(lengths, queries, keys, values):
    rows, width = queries.shape
    return pl.pallas_call(
        attention_kernel,
        out_shape=jax.ShapeDtypeStruct((rows, width), BF16),
        in_specs=[ANY] * 4,
        out_specs=VMEM,
        scratch_shapes=[
            pltpu.SMEM(lengths.shape, jnp.int32),
            pltpu.VMEM((rows, width), BF16),
            pltpu.VMEM(keys.shape, BF16),
            pltpu.VMEM(values.shape, BF16),
            pltpu.VMEM((rows * width // HEAD, HEAD), F32),
            pltpu.VMEM((rows, width), F32),
            pltpu.SemaphoreType.DMA((2 + 2 * rows,)),
        ],
        compiler_params=params(16),
        name="attention",
    )(*map(in_hbm, (lengths, queries, keys, values)))


def join_kernel(a_ref, b_ref, out_ref):
    rows = a_ref.shape[0]
    out_ref[:rows] = a_ref[...]
    out_ref[rows:] = b_ref[...]


def join(a, b):
    return pl.pallas_call(
        join_kernel,
        out_shape=jax.ShapeDtypeStruct((a.shape[0] + b.shape[0],) + a.shape[1:], a.dtype),
        in_specs=[VMEM] * 2,
        out_specs=VMEM,
        compiler_params=params(1),
        name="join",
    )(a, b)


def in_hbm(value):
    return pltpu.with_memory_space_constraint(value, pltpu.HBM)


def fetch_kernel(*refs):
    count = (len(refs) - 2) // 2
    sources, targets, sems = refs[1 : 1 + count], refs[1 + count : -1], refs[-1]
    copies = [
        pltpu.make_async_copy(s, t, sems.at[i]) for i, (s, t) in enumerate(zip(sources, targets))
    ]
    for copy in copies:
        copy.start()
    for copy in copies:
        copy.wait()


def fetch(after, *arrays):
    size = sum(a.size * a.dtype.itemsize for a in arrays)
    return pl.pallas_call(
        fetch_kernel,
        out_shape=[pltpu.VMEM(a.shape, a.dtype) for a in arrays],
        in_specs=[ANY] * (1 + len(arrays)),
        out_specs=[VMEM] * len(arrays),
        scratch_shapes=[pltpu.SemaphoreType.DMA((len(arrays),))],
        compiler_params=params(1),
        cost_estimate=pl.CostEstimate(flops=0, bytes_accessed=size, transcendentals=0),
        name="fetch",
    )(after, *map(in_hbm, arrays))


def routes_of(ids, weights):
    top = ids.shape[0]
    lane = lax.broadcasted_iota(jnp.int32, (ROWS, LANES), 1)
    row = lax.broadcasted_iota(jnp.int32, (ROWS, LANES), 0)
    hi, mid, lo = split3(weights)
    total = jnp.zeros((top, LANES), F32)
    for piece, start in ((ids.astype(F32), IDS), (hi, HI), (mid, MID), (lo, LO)):
        place = (lane == row + start).astype(BF16)
        total += jnp.dot(piece.astype(BF16), place, preferred_element_type=F32)
    return total


def stream_kernel(
    a0, a1, a2, a3, w_ref, residual_ref, gain_ref, ids_ref, weights_ref, stream_ref, unit_ref, rows_ref
):
    part = a0.shape[0]
    for k, a in enumerate((a0, a1, a2, a3)):
        rows_ref[k * part : (k + 1) * part, :] = a[...].astype(F32)
    mixed = jnp.dot(rows_ref[...].astype(BF16), w_ref[...], preferred_element_type=F32)
    half = part // CORES
    z, c = lax.axis_index("z"), lax.axis_index("c")
    here = lax.broadcasted_iota(jnp.int32, (ROWS, ROWS), 1)
    wanted = lax.broadcasted_iota(jnp.int32, (ROWS, ROWS), 0)
    slot, within = here // part, here % part
    owner = (z - slot + SIDE) % SIDE * CORES + (c + within // half) % CORES
    order = (wanted == owner * half + within % half).astype(F32)
    mixed = jnp.dot(order, mixed, precision=lax.Precision.HIGHEST, preferred_element_type=F32)
    stream = (residual_ref[...].astype(F32) + mixed).astype(BF16)
    stream_ref[...] = stream
    widened = stream.astype(F32)
    scaled = (widened * gain_ref[...]).astype(BF16)
    squares = jnp.sum(widened * widened, axis=1, keepdims=True)
    lane = lax.broadcasted_iota(jnp.int32, (ROWS, LANES), 1)
    row = lax.broadcasted_iota(jnp.int32, (ROWS, LANES), 0)
    squares = jnp.sum(jnp.where(lane == row + SQ, squares, 0.0), axis=0, keepdims=True)
    extra = routes_of(ids_ref[...], weights_ref[...])
    line = lax.broadcasted_iota(jnp.int32, extra.shape, 0)
    held = lax.broadcasted_iota(jnp.int32, extra.shape, 1) >= SQ
    for i, piece in enumerate(split3(squares)):
        extra = jnp.where(held & (line == i), piece, extra)
    unit = jnp.concatenate(
        [scaled[:, j * LANES : (j + 1) * LANES] for j in range(CHUNKS)] + [extra.astype(BF16)],
        axis=0,
    )
    for i in range(unit_ref.shape[0]):
        unit_ref[i] = unit


def make_stream(parts, out_proj, residual, gain, ids, weights):
    return pl.pallas_call(
        stream_kernel,
        out_shape=[
            jax.ShapeDtypeStruct((ROWS, COLS), BF16),
            jax.ShapeDtypeStruct((PLACES * SIDE, UNIT + EXTRA, LANES), BF16),
        ],
        in_specs=[VMEM] * 9,
        out_specs=[VMEM, VMEM],
        scratch_shapes=[pltpu.VMEM((ROWS, D), F32)],
        compiler_params=params(4),
        cost_estimate=pl.CostEstimate(
            flops=10000000000, bytes_accessed=60000000, transcendentals=0
        ),
        name="stream",
    )(*parts, out_proj, residual, gain, ids, weights)


def to_columns(lines, start):
    shape = (PLACES, ROWS, LANES)
    lane = lax.broadcasted_iota(jnp.int32, shape, 2)
    row = lax.broadcasted_iota(jnp.int32, shape, 1)
    kept = jnp.where(lane == row + start, jnp.broadcast_to(lines, shape), 0.0)
    return jnp.sum(kept, axis=2, keepdims=True).reshape(PLACES * ROWS, 1)


def gather_rows(units_ref, x_ref):
    for s in range(PLACES):
        for z in range(SIDE):
            for j in range(CHUNKS):
                start = z * COLS + j * LANES
                x_ref[s * ROWS : (s + 1) * ROWS, start : start + LANES] = units_ref[
                    RANK[s * SIDE + z], j * ROWS : (j + 1) * ROWS, :
                ]


def columns_of(z, parity):
    return pl.ds(pl.multiple_of((z * CORES + parity) * COLS, COLS), COLS)


def products(x_ref, w_ref, parity, first=0, count=None):
    count = count or w_ref.shape[0]
    total = None
    for z in range(SIDE):
        part = lax.dot_general(
            x_ref[:, z * COLS : (z + 1) * COLS],
            w_ref[first : first + count, columns_of(z, parity)],
            NT,
            preferred_element_type=F32,
        )
        total = part if total is None else total + part
    return total


def squares_of(units):
    extras = jnp.sum(units[:, UNIT : UNIT + 3, :].astype(F32), axis=1, keepdims=True)
    return sum(
        jnp.stack([extras[RANK[s * SIDE + z]] for s in range(PLACES)]) for z in range(SIDE)
    )


def own_kernel(own_ref, gate_ref, up_ref, down_ref, gate_sum, up_sum, mix_ref, squares_ref, x_ref):
    c = lax.axis_index("c")
    gather_rows(own_ref, x_ref)
    squares_ref[...] = squares_of(own_ref)
    routes = jnp.stack([own_ref[RANK[s * SIDE], UNIT:, :] for s in range(PLACES)]).astype(F32)
    weights = (
        pltpu.roll(routes, LANES - HI, 2)
        + pltpu.roll(routes, LANES - MID, 2)
        + pltpu.roll(routes, LANES - LO, 2)
    )
    local = gate_ref.shape[0] // EXPERT_COLS
    first = (lax.axis_index("x") * SIDE + lax.axis_index("y")) * local
    column = lax.broadcasted_iota(jnp.int32, mix_ref.shape, 1)
    mix = None
    for e in range(local):
        mine = jnp.where(routes == (first + e).astype(F32), weights, 0.0)
        one = to_columns(jnp.sum(mine, axis=1, keepdims=True), IDS)
        mix = one if mix is None else jnp.where(column < e * EXPERT_COLS, mix, one)
    mix_ref[...] = mix
    gate_sum[...] = products(x_ref, gate_ref, c)
    up_sum[...] = products(x_ref, up_ref, c)


def own_part(own, gate, up, down):
    rows = PLACES * ROWS
    width = gate.shape[0]
    return pl.pallas_call(
        own_kernel,
        out_shape=[jax.ShapeDtypeStruct((rows, width), F32)] * 3
        + [jax.ShapeDtypeStruct((PLACES, 1, LANES), F32)],
        in_specs=[VMEM] * 4,
        out_specs=[VMEM] * 4,
        scratch_shapes=[pltpu.VMEM((rows, D // CORES), BF16)],
        compiler_params=params(8),
        name="own_part",
    )(own, gate, up, down)


PARTS = 3


def hidden_kernel(
    other_ref, gate_ref, up_ref, gate_in, up_in, mix_ref, squares_ref, down_ref, hidden_ref, out_ref, x_ref
):
    other = 1 - lax.axis_index("c")
    gather_rows(other_ref, x_ref)
    scale = lax.rsqrt(to_columns(squares_ref[...] + squares_of(other_ref), SQ) / D + 1e-06)
    width = hidden_ref.shape[1] // PARTS
    for i in range(PARTS):
        first = i * width
        part = slice(first, first + width)
        half = (gate_in[:, part] + products(x_ref, gate_ref, other, first, width)) * (0.5 * scale)
        up = (up_in[:, part] + products(x_ref, up_ref, other, first, width)) * scale
        hidden_ref[:, part] = ((half + half * jnp.tanh(half)) * up * mix_ref[:, part]).astype(BF16)
    down_part(hidden_ref, down_ref, other, out_ref)


def down_part(hidden_ref, down_ref, parity, out_ref):
    for z in range(SIDE):
        part = jnp.dot(
            hidden_ref[...],
            down_ref[:, columns_of(z, parity)],
            preferred_element_type=F32,
        ).astype(BF16)
        for s in range(PLACES):
            out_ref[s, z] = part[s * ROWS : (s + 1) * ROWS]


def blocks(count):
    return jax.ShapeDtypeStruct((PLACES, count, ROWS, COLS), BF16)


def make_hidden(other, gate, up, sums, down):
    rows = PLACES * ROWS
    width = gate.shape[0]
    return pl.pallas_call(
        hidden_kernel,
        out_shape=[jax.ShapeDtypeStruct((rows, width), BF16), blocks(SIDE)],
        in_specs=[VMEM] * 8,
        out_specs=[VMEM] * 2,
        scratch_shapes=[pltpu.VMEM((rows, D // CORES), BF16)],
        compiler_params=params(12),
        name="hidden",
    )(other, gate, up, *sums, down)


def down_kernel(hidden_ref, down_ref, out_ref):
    down_part(hidden_ref, down_ref, lax.axis_index("c"), out_ref)


def down_blocks(hidden, down):
    return pl.pallas_call(
        down_kernel,
        out_shape=blocks(SIDE),
        in_specs=[VMEM, VMEM],
        out_specs=VMEM,
        compiler_params=params(4),
        name="down_mine",
    )(hidden, down)


def add_kernel(mine_ref, came_ref, out_ref):
    for z in range(SIDE):
        total = mine_ref[:, z].astype(F32) + came_ref[:, z].astype(F32)
        for s in range(PLACES):
            out_ref[RANK[s * SIDE + z]] = total[s].astype(BF16)


def add(mine, came):
    return pl.pallas_call(
        add_kernel,
        out_shape=jax.ShapeDtypeStruct((PLACES * SIDE, ROWS, COLS), BF16),
        in_specs=[VMEM] * 2,
        out_specs=VMEM,
        compiler_params=params(4),
        name="add",
    )(mine, came)


def finish_kernel(parts_ref, stream_ref, out_hbm, out_ref, sem):
    total = stream_ref[...].astype(F32)
    for i in range(parts_ref.shape[0]):
        total += parts_ref[i].astype(F32)
    out_ref[...] = total.astype(BF16)
    copy = pltpu.make_async_copy(out_ref, out_hbm, sem)
    copy.start()
    copy.wait()


def finish(parts, stream):
    return pl.pallas_call(
        finish_kernel,
        out_shape=jax.ShapeDtypeStruct(stream.shape, BF16),
        in_specs=[VMEM] * 2,
        out_specs=ANY,
        scratch_shapes=[pltpu.VMEM(stream.shape, BF16), pltpu.SemaphoreType.DMA],
        compiler_params=params(4),
        name="finish",
    )(parts, stream)


def exchange(blocks):
    axes = ("x", "y", "z", "c")
    return lax.all_to_all(
        blocks, axes, split_axis=0, concat_axis=0, axis_index_groups=GROUPS, tiled=True
    )


def on_device(
    queries,
    key_cache,
    value_cache,
    lengths,
    residual,
    out_proj,
    norm_gain,
    expert_ids,
    route_weights,
    w_gate,
    w_up,
    w_down,
):
    gate = jnp.swapaxes(w_gate, 1, 2).reshape(-1, D)
    up = jnp.swapaxes(w_up, 1, 2).reshape(-1, D)
    down = w_down.reshape(-1, D)
    attended = attention(lengths, queries, key_cache, value_cache)
    pair = join(attended, swap(attended))
    parts = spread_z(pair)
    residual, gain, ids, weights, out_proj = fetch(
        pair, residual, norm_gain[None, :], expert_ids.T, route_weights.T, out_proj
    )
    stream, units = make_stream(parts, out_proj, residual, gain, ids, weights)
    own = exchange(units)
    other = swap(own)
    sums = own_part(own, gate, up, down)
    hidden, theirs = make_hidden(other, gate, up, sums, down)
    came = swap(theirs)
    mine = down_blocks(hidden, down)
    return finish(exchange(add(mine, came)), stream)


def solution(mesh):
    devices = mesh.devices.reshape(SIDE, SIDE, SIDE, CORES)
    pool, grp = ("x", "y"), ("z", "c")
    every = pool + grp
    in_specs = (
        P(every, None),
        P(every, None, None),
        P(every, None, None),
        P(every),
        P(pool, grp),
        P(None, grp),
        P(grp),
        P(pool, None),
        P(pool, None),
        P(pool, None, grp),
        P(pool, None, grp),
        P(pool, grp, None),
    )
    return jax.shard_map(
        on_device,
        mesh=Mesh(devices, every),
        in_specs=in_specs,
        out_specs=P(pool, grp),
        check_vma=False,
    )
```

```python
import functools
import math
import random

import jax
import jax.numpy as jnp
from jax import lax
from jax.experimental import pallas as pl
from jax.experimental.pallas import tpu as pltpu
from jax.sharding import Mesh
from jax.sharding import PartitionSpec as P

D = 4096
KV_HEADS = 2
HEAD = 128
LANES = 128
SIDE = 4
CORES = 2
PLACES = SIDE * SIDE
COLS = D // (SIDE * CORES)
CHUNKS = COLS // LANES
ROWS = 16
UNIT = CHUNKS * ROWS
EXTRA = 8
IDS, HI, MID, LO, SQ = 0, ROWS, 2 * ROWS, 3 * ROWS, 4 * ROWS
EXPERT_COLS = 192
ORDER = list(range(PLACES * SIDE))
random.Random(13).shuffle(ORDER)
RANK = [ORDER.index(place) for place in range(PLACES * SIDE)]
GROUPS = [[place * CORES + c for place in ORDER] for c in range(CORES)]
F32 = jnp.float32
BF16 = jnp.bfloat16
NT = (((1,), (1,)), ((), ()))
VMEM = pl.BlockSpec(memory_space=pltpu.VMEM)
ANY = pl.BlockSpec(memory_space=pl.ANY)


def params(mib):
    return pltpu.CompilerParams(vmem_limit_bytes=mib * 1024 * 1024)


def split3(value):
    hi = value.astype(BF16).astype(F32)
    mid = (value - hi).astype(BF16).astype(F32)
    lo = value - hi - mid
    return hi, mid, lo


SWAP = [(0, 1), (1, 0)]


def swap(block):
    return lax.ppermute(block, "c", SWAP)


def spread_z(block):
    return [block] + [
        lax.ppermute(block, "z", [(i, (i + k) % SIDE) for i in range(SIDE)])
        for k in range(1, SIDE)
    ]


def attention_kernel(
    len_hbm, q_hbm, k_hbm, v_hbm, out_ref, lens, q_ref, k_ref, v_ref, q_rows, out_rows, sems
):
    rows, width = q_ref.shape
    positions = k_ref.shape[1]
    heads = width // HEAD
    per_group = heads // KV_HEADS
    len_copy = pltpu.make_async_copy(len_hbm, lens, sems.at[0])
    q_copy = pltpu.make_async_copy(q_hbm, q_ref, sems.at[1])
    k_copies = [
        pltpu.make_async_copy(k_hbm.at[r], k_ref.at[r], sems.at[2 + r]) for r in range(rows)
    ]
    v_copies = [
        pltpu.make_async_copy(v_hbm.at[r], v_ref.at[r], sems.at[2 + rows + r])
        for r in range(rows)
    ]
    q_copy.start()
    len_copy.start()
    for copy in k_copies + v_copies:
        copy.start()
    q_copy.wait()
    queries = q_ref[...].astype(F32)
    for r in range(rows):
        for h in range(heads):
            q_rows[r * heads + h : r * heads + h + 1, :] = queries[
                r : r + 1, h * HEAD : (h + 1) * HEAD
            ]
    len_copy.wait()
    spots = lax.broadcasted_iota(jnp.int32, (per_group, positions), 1)
    cases = [(r, g) for r in range(rows) for g in range(KV_HEADS)]
    for copy in k_copies:
        copy.wait()
    scores = []
    for r, g in cases:
        first = r * heads + g * per_group
        q = q_rows[first : first + per_group, :].astype(BF16)
        keys = k_ref[r, :, g * HEAD : (g + 1) * HEAD]
        product = lax.dot_general(q, keys, NT, preferred_element_type=F32) / math.sqrt(HEAD)
        scores.append(jnp.where(spots < lens[r], product, -1e30))
    peaks = [jnp.max(x, axis=1, keepdims=True) for x in scores]
    probs = [
        jnp.where(spots < lens[r], jnp.exp(x - peak), 0.0)
        for (r, g), x, peak in zip(cases, scores, peaks)
    ]
    sums = [jnp.sum(x, axis=1, keepdims=True) for x in probs]
    for copy in v_copies:
        copy.wait()
    for (r, g), x, weight_sum in zip(cases, probs, sums):
        values = v_ref[r, :, g * HEAD : (g + 1) * HEAD]
        summed = jnp.dot(x.astype(BF16), values, preferred_element_type=F32) / weight_sum
        for j in range(per_group):
            h = g * per_group + j
            out_rows[r : r + 1, h * HEAD : (h + 1) * HEAD] = summed[j : j + 1, :]
    out_ref[...] = out_rows[...].astype(BF16)


def attention(lengths, queries, keys, values):
    rows, width = queries.shape
    return pl.pallas_call(
        attention_kernel,
        out_shape=jax.ShapeDtypeStruct((rows, width), BF16),
        in_specs=[ANY] * 4,
        out_specs=VMEM,
        scratch_shapes=[
            pltpu.SMEM(lengths.shape, jnp.int32),
            pltpu.VMEM((rows, width), BF16),
            pltpu.VMEM(keys.shape, BF16),
            pltpu.VMEM(values.shape, BF16),
            pltpu.VMEM((rows * width // HEAD, HEAD), F32),
            pltpu.VMEM((rows, width), F32),
            pltpu.SemaphoreType.DMA((2 + 2 * rows,)),
        ],
        compiler_params=params(16),
        name="attention",
    )(*map(in_hbm, (lengths, queries, keys, values)))


def join_kernel(a_ref, b_ref, out_ref):
    rows = a_ref.shape[0]
    out_ref[:rows] = a_ref[...]
    out_ref[rows:] = b_ref[...]


def join(a, b):
    return pl.pallas_call(
        join_kernel,
        out_shape=jax.ShapeDtypeStruct((a.shape[0] + b.shape[0],) + a.shape[1:], a.dtype),
        in_specs=[VMEM] * 2,
        out_specs=VMEM,
        compiler_params=params(1),
        name="join",
    )(a, b)


def in_hbm(value):
    return pltpu.with_memory_space_constraint(value, pltpu.HBM)


def fetch_kernel(*refs):
    count = (len(refs) - 2) // 2
    sources, targets, sems = refs[1 : 1 + count], refs[1 + count : -1], refs[-1]
    copies = [
        pltpu.make_async_copy(s, t, sems.at[i]) for i, (s, t) in enumerate(zip(sources, targets))
    ]
    for copy in copies:
        copy.start()
    for copy in copies:
        copy.wait()


def fetch(after, *arrays):
    size = sum(a.size * a.dtype.itemsize for a in arrays)
    return pl.pallas_call(
        fetch_kernel,
        out_shape=[pltpu.VMEM(a.shape, a.dtype) for a in arrays],
        in_specs=[ANY] * (1 + len(arrays)),
        out_specs=[VMEM] * len(arrays),
        scratch_shapes=[pltpu.SemaphoreType.DMA((len(arrays),))],
        compiler_params=params(1),
        cost_estimate=pl.CostEstimate(flops=0, bytes_accessed=size, transcendentals=0),
        name="fetch",
    )(after, *map(in_hbm, arrays))


def routes_of(ids, weights):
    top = ids.shape[0]
    lane = lax.broadcasted_iota(jnp.int32, (ROWS, LANES), 1)
    row = lax.broadcasted_iota(jnp.int32, (ROWS, LANES), 0)
    hi, mid, lo = split3(weights)
    total = jnp.zeros((top, LANES), F32)
    for piece, start in ((ids.astype(F32), IDS), (hi, HI), (mid, MID), (lo, LO)):
        place = (lane == row + start).astype(BF16)
        total += jnp.dot(piece.astype(BF16), place, preferred_element_type=F32)
    return total


def stream_kernel(
    a0, a1, a2, a3, w_ref, residual_ref, gain_ref, ids_ref, weights_ref, stream_ref, unit_ref, rows_ref
):
    part = a0.shape[0]
    for k, a in enumerate((a0, a1, a2, a3)):
        rows_ref[k * part : (k + 1) * part, :] = a[...].astype(F32)
    mixed = jnp.dot(rows_ref[...].astype(BF16), w_ref[...], preferred_element_type=F32)
    half = part // CORES
    z, c = lax.axis_index("z"), lax.axis_index("c")
    here = lax.broadcasted_iota(jnp.int32, (ROWS, ROWS), 1)
    wanted = lax.broadcasted_iota(jnp.int32, (ROWS, ROWS), 0)
    slot, within = here // part, here % part
    owner = (z - slot + SIDE) % SIDE * CORES + (c + within // half) % CORES
    order = (wanted == owner * half + within % half).astype(F32)
    mixed = jnp.dot(order, mixed, precision=lax.Precision.HIGHEST, preferred_element_type=F32)
    stream = (residual_ref[...].astype(F32) + mixed).astype(BF16)
    stream_ref[...] = stream
    widened = stream.astype(F32)
    scaled = (widened * gain_ref[...]).astype(BF16)
    squares = jnp.sum(widened * widened, axis=1, keepdims=True)
    lane = lax.broadcasted_iota(jnp.int32, (ROWS, LANES), 1)
    row = lax.broadcasted_iota(jnp.int32, (ROWS, LANES), 0)
    squares = jnp.sum(jnp.where(lane == row + SQ, squares, 0.0), axis=0, keepdims=True)
    extra = routes_of(ids_ref[...], weights_ref[...])
    line = lax.broadcasted_iota(jnp.int32, extra.shape, 0)
    held = lax.broadcasted_iota(jnp.int32, extra.shape, 1) >= SQ
    for i, piece in enumerate(split3(squares)):
        extra = jnp.where(held & (line == i), piece, extra)
    unit = jnp.concatenate(
        [scaled[:, j * LANES : (j + 1) * LANES] for j in range(CHUNKS)] + [extra.astype(BF16)],
        axis=0,
    )
    for i in range(unit_ref.shape[0]):
        unit_ref[i] = unit


def make_stream(parts, out_proj, residual, gain, ids, weights):
    return pl.pallas_call(
        stream_kernel,
        out_shape=[
            jax.ShapeDtypeStruct((ROWS, COLS), BF16),
            jax.ShapeDtypeStruct((PLACES * SIDE, UNIT + EXTRA, LANES), BF16),
        ],
        in_specs=[VMEM] * 9,
        out_specs=[VMEM, VMEM],
        scratch_shapes=[pltpu.VMEM((ROWS, D), F32)],
        compiler_params=params(4),
        cost_estimate=pl.CostEstimate(
            flops=10000000000, bytes_accessed=60000000, transcendentals=0
        ),
        name="stream",
    )(*parts, out_proj, residual, gain, ids, weights)


def to_columns(lines, start):
    shape = (PLACES, ROWS, LANES)
    lane = lax.broadcasted_iota(jnp.int32, shape, 2)
    row = lax.broadcasted_iota(jnp.int32, shape, 1)
    kept = jnp.where(lane == row + start, jnp.broadcast_to(lines, shape), 0.0)
    return jnp.sum(kept, axis=2, keepdims=True).reshape(PLACES * ROWS, 1)


def gather_rows(units_ref, x_ref):
    for s in range(PLACES):
        for z in range(SIDE):
            for j in range(CHUNKS):
                start = z * COLS + j * LANES
                x_ref[s * ROWS : (s + 1) * ROWS, start : start + LANES] = units_ref[
                    RANK[s * SIDE + z], j * ROWS : (j + 1) * ROWS, :
                ]


def columns_of(z, parity):
    return pl.ds(pl.multiple_of((z * CORES + parity) * COLS, COLS), COLS)


def products(x_ref, w_ref, parity, first=0, count=None):
    count = count or w_ref.shape[0]
    total = None
    for z in range(SIDE):
        part = lax.dot_general(
            x_ref[:, z * COLS : (z + 1) * COLS],
            w_ref[first : first + count, columns_of(z, parity)],
            NT,
            preferred_element_type=F32,
        )
        total = part if total is None else total + part
    return total


def squares_of(units):
    extras = jnp.sum(units[:, UNIT : UNIT + 3, :].astype(F32), axis=1, keepdims=True)
    return sum(
        jnp.stack([extras[RANK[s * SIDE + z]] for s in range(PLACES)]) for z in range(SIDE)
    )


def own_kernel(own_ref, gate_ref, up_ref, down_ref, gate_sum, up_sum, mix_ref, squares_ref, x_ref):
    c = lax.axis_index("c")
    gather_rows(own_ref, x_ref)
    squares_ref[...] = squares_of(own_ref)
    routes = jnp.stack([own_ref[RANK[s * SIDE], UNIT:, :] for s in range(PLACES)]).astype(F32)
    weights = (
        pltpu.roll(routes, LANES - HI, 2)
        + pltpu.roll(routes, LANES - MID, 2)
        + pltpu.roll(routes, LANES - LO, 2)
    )
    local = gate_ref.shape[0] // EXPERT_COLS
    first = (lax.axis_index("x") * SIDE + lax.axis_index("y")) * local
    column = lax.broadcasted_iota(jnp.int32, mix_ref.shape, 1)
    mix = None
    for e in range(local):
        mine = jnp.where(routes == (first + e).astype(F32), weights, 0.0)
        one = to_columns(jnp.sum(mine, axis=1, keepdims=True), IDS)
        mix = one if mix is None else jnp.where(column < e * EXPERT_COLS, mix, one)
    mix_ref[...] = mix
    gate_sum[...] = products(x_ref, gate_ref, c)
    up_sum[...] = products(x_ref, up_ref, c)


def own_part(own, gate, up, down):
    rows = PLACES * ROWS
    width = gate.shape[0]
    return pl.pallas_call(
        own_kernel,
        out_shape=[jax.ShapeDtypeStruct((rows, width), F32)] * 3
        + [jax.ShapeDtypeStruct((PLACES, 1, LANES), F32)],
        in_specs=[VMEM] * 4,
        out_specs=[VMEM] * 4,
        scratch_shapes=[pltpu.VMEM((rows, D // CORES), BF16)],
        compiler_params=params(8),
        name="own_part",
    )(own, gate, up, down)


PARTS = 3


def hidden_kernel(
    other_ref, gate_ref, up_ref, gate_in, up_in, mix_ref, squares_ref, down_ref, hidden_ref, out_ref, x_ref
):
    other = 1 - lax.axis_index("c")
    gather_rows(other_ref, x_ref)
    scale = lax.rsqrt(to_columns(squares_ref[...] + squares_of(other_ref), SQ) / D + 1e-06)
    width = hidden_ref.shape[1] // PARTS
    for i in range(PARTS):
        first = i * width
        part = slice(first, first + width)
        half = (gate_in[:, part] + products(x_ref, gate_ref, other, first, width)) * (0.5 * scale)
        up = (up_in[:, part] + products(x_ref, up_ref, other, first, width)) * scale
        hidden_ref[:, part] = ((half + half * jnp.tanh(half)) * up * mix_ref[:, part]).astype(BF16)
    down_part(hidden_ref, down_ref, other, out_ref)


def down_part(hidden_ref, down_ref, parity, out_ref):
    for z in range(SIDE):
        part = jnp.dot(
            hidden_ref[...],
            down_ref[:, columns_of(z, parity)],
            preferred_element_type=F32,
        ).astype(BF16)
        for s in range(PLACES):
            out_ref[s, z] = part[s * ROWS : (s + 1) * ROWS]


def blocks(count):
    return jax.ShapeDtypeStruct((PLACES, count, ROWS, COLS), BF16)


def make_hidden(other, gate, up, sums, down):
    rows = PLACES * ROWS
    width = gate.shape[0]
    return pl.pallas_call(
        hidden_kernel,
        out_shape=[jax.ShapeDtypeStruct((rows, width), BF16), blocks(SIDE)],
        in_specs=[VMEM] * 8,
        out_specs=[VMEM] * 2,
        scratch_shapes=[pltpu.VMEM((rows, D // CORES), BF16)],
        compiler_params=params(12),
        name="hidden",
    )(other, gate, up, *sums, down)


def down_kernel(hidden_ref, down_ref, out_ref):
    down_part(hidden_ref, down_ref, lax.axis_index("c"), out_ref)


def down_blocks(hidden, down):
    return pl.pallas_call(
        down_kernel,
        out_shape=blocks(SIDE),
        in_specs=[VMEM, VMEM],
        out_specs=VMEM,
        compiler_params=params(4),
        name="down_mine",
    )(hidden, down)


def add_kernel(mine_ref, came_ref, out_ref):
    for z in range(SIDE):
        total = mine_ref[:, z].astype(F32) + came_ref[:, z].astype(F32)
        for s in range(PLACES):
            out_ref[RANK[s * SIDE + z]] = total[s].astype(BF16)


def add(mine, came):
    return pl.pallas_call(
        add_kernel,
        out_shape=jax.ShapeDtypeStruct((PLACES * SIDE, ROWS, COLS), BF16),
        in_specs=[VMEM] * 2,
        out_specs=VMEM,
        compiler_params=params(4),
        name="add",
    )(mine, came)


def finish_kernel(parts_ref, stream_ref, out_hbm, out_ref, sem):
    total = stream_ref[...].astype(F32)
    for i in range(parts_ref.shape[0]):
        total += parts_ref[i].astype(F32)
    out_ref[...] = total.astype(BF16)
    copy = pltpu.make_async_copy(out_ref, out_hbm, sem)
    copy.start()
    copy.wait()


def finish(parts, stream):
    return pl.pallas_call(
        finish_kernel,
        out_shape=jax.ShapeDtypeStruct(stream.shape, BF16),
        in_specs=[VMEM] * 2,
        out_specs=ANY,
        scratch_shapes=[pltpu.VMEM(stream.shape, BF16), pltpu.SemaphoreType.DMA],
        compiler_params=params(4),
        name="finish",
    )(parts, stream)


def exchange(blocks):
    axes = ("x", "y", "z", "c")
    return lax.all_to_all(
        blocks, axes, split_axis=0, concat_axis=0, axis_index_groups=GROUPS, tiled=True
    )


def on_device(
    queries,
    key_cache,
    value_cache,
    lengths,
    residual,
    out_proj,
    norm_gain,
    expert_ids,
    route_weights,
    w_gate,
    w_up,
    w_down,
):
    gate = jnp.swapaxes(w_gate, 1, 2).reshape(-1, D)
    up = jnp.swapaxes(w_up, 1, 2).reshape(-1, D)
    down = w_down.reshape(-1, D)
    attended = attention(lengths, queries, key_cache, value_cache)
    pair = join(attended, swap(attended))
    parts = spread_z(pair)
    residual, gain, ids, weights, out_proj = fetch(
        pair, residual, norm_gain[None, :], expert_ids.T, route_weights.T, out_proj
    )
    stream, units = make_stream(parts, out_proj, residual, gain, ids, weights)
    own = exchange(units)
    other = swap(own)
    sums = own_part(own, gate, up, down)
    hidden, theirs = make_hidden(other, gate, up, sums, down)
    came = swap(theirs)
    mine = down_blocks(hidden, down)
    return finish(exchange(add(mine, came)), stream)


def solution(mesh):
    devices = mesh.devices.reshape(SIDE, SIDE, SIDE, CORES)
    pool, grp = ("x", "y"), ("z", "c")
    every = pool + grp
    in_specs = (
        P(every, None),
        P(every, None, None),
        P(every, None, None),
        P(every),
        P(pool, grp),
        P(None, grp),
        P(grp),
        P(pool, None),
        P(pool, None),
        P(pool, None, grp),
        P(pool, None, grp),
        P(pool, grp, None),
    )
    return jax.shard_map(
        on_device,
        mesh=Mesh(devices, every),
        in_specs=in_specs,
        out_specs=P(pool, grp),
        check_vma=False,
    )
```
